512 devices in a mesh: row: 32 (over x_hi, z, core), col: 16 (over x_lo, y).
Axes of the slice: x: 4 (x_hi: 2, x_lo: 2; x = x_hi * 2 + x_lo), y: 8, z: 8, core: 2. Of those that a mesh axis runs over, the one named last changes fastest.
Arguments:
- pair: bfloat16 [512, 512, 128], P('row', 'col'), may hold values from -6 to 6
- w_proj: bfloat16 [128, 512], replicated
- w_bias: bfloat16 [128, 4], replicated, may hold values from -0.5 to 0.5
- w_out: bfloat16 [128, 128], replicated, may hold values from -0.5 to 0.5
- token_mask: int32 [512], P('col'), may hold values from 0 to 1, as said below
Outputs:
- update: bfloat16 [512, 512, 128], P('row', 'col')
The draws below stay inside these ranges and needn't reach their ends.
Inputs may be any that keep to these rules, and one draw needn't show every extreme that they name: `token_mask`: token 0 is real; the last 32 tokens or more are padding; real tokens before the padding have gaps.
All inputs are finite; a program needn't handle non-finite values.
Results may differ from the reference program's by a relative error of at most 0.011.
The reference program's roundings to bfloat16 on the way (of `pair`, `normed`, `query`, `bias`, `weights` and `gated`) count: a program that leaves them out, or rounds other values in their place, can miss the bound.
Values may be sent and summed in bfloat16 or wider, within the bound.
No kernel may reach another device: no remote copies, remote signals or barrier semaphores. Data moves between devices by JAX's collectives and lax.ppermute only.
A program may use at most 128 MiB of HBM per device.

```python
import jax
import jax.numpy as jnp
from jax import lax

D = 128
H = 4
C = 32
N = 512


def draw_w_proj(key, part):
    key = jax.random.fold_in(key, 7)
    weights = jax.random.normal(key, (D, 4 * D), jnp.float32) * D ** (-0.5)
    return weights.astype(jnp.bfloat16)


def draw_token_mask(key, part):
    key = jax.random.fold_in(key, 5)
    first_key, second_key = jax.random.split(key)
    length = jax.random.randint(first_key, (), N // 2, N - C + 1)
    position = jnp.arange(N, dtype=jnp.int32)
    holes = jax.random.randint(second_key, (N,), 0, 8)
    valid = (position < length) & ((holes != 0) | (position == 0))
    return valid.astype(jnp.int32)


def steps_of(own_key, extent, shards, least, largest):
    gain = 1.0
    for dim, parts in shards:
        steps = jax.random.uniform(jax.random.fold_in(jax.random.fold_in(own_key, 6), dim), (parts,), jnp.float32, least / len(shards), largest / len(shards))
        gain = gain * jnp.repeat(jnp.exp(steps), extent[dim] // parts).reshape((-1,) + (1,) * (len(extent) - 1 - dim))
    return gain


def centred(key, shape, deviation, most, cuts=(), kind=jnp.bfloat16):
    entries = jax.random.normal(key, shape, jnp.float32) * deviation
    if len(cuts) > 0:
        entries = steps_of(key, shape, cuts, -0.22, 0.18) * entries
    return jnp.clip(entries, min=-most, max=most).astype(kind)


def setup_inputs(seed: int = 0) -> dict:
    seeds = jax.random.split(jax.random.key(seed), 6)
    return {
        "pair": centred(seeds[0], (N, N, D), 1.0, 6.0, ((0, 32), (1, 16))),
        "w_proj": draw_w_proj(jax.random.fold_in(seeds[5], 71), 0),
        "w_bias": centred(seeds[2], (D, H), D ** -0.5, 0.5),
        "w_out": centred(seeds[3], (D, D), D ** -0.5, 0.5),
        "token_mask": draw_token_mask(jax.random.fold_in(seeds[5], 71), 0),
    }


def norm_rows(block):
    values = block.astype(jnp.float32)
    center = lax.optimization_barrier(jnp.mean(values, axis=-1, keepdims=True))
    spread = lax.optimization_barrier(jnp.mean((values - center) ** 2, axis=-1, keepdims=True))
    return ((values - center) * lax.rsqrt(spread + 1e-05)).astype(jnp.bfloat16)

def reference(pair, w_proj, w_bias, w_out, token_mask):
    width = pair.shape[2]
    heads = w_bias.shape[1]
    head_size = width // heads
    count = pair.shape[0]

    def bias_row(row):
        return jnp.dot(norm_rows(row), w_bias, preferred_element_type=jnp.float32).astype(jnp.bfloat16)
    bias = lax.map(bias_row, pair)
    bias_heads = jnp.transpose(bias, (2, 0, 1)).astype(jnp.float32)
    masked = (token_mask.astype(jnp.float32) - 1.0) * 1000000000.0

    def one_row(row):
        normed = norm_rows(row)
        proj = jnp.dot(normed, w_proj, preferred_element_type=jnp.float32)
        query = (proj[:, :width] * head_size ** (-0.5)).astype(jnp.bfloat16).reshape(count, heads, head_size)
        keys = proj[:, width:2 * width].astype(jnp.bfloat16).reshape(count, heads, head_size)
        values = proj[:, 2 * width:3 * width].astype(jnp.bfloat16).reshape(count, heads, head_size)
        gates = proj[:, 3 * width:].astype(jnp.bfloat16)
        scores = jnp.einsum('jhd,khd->hjk', query.astype(jnp.float32), keys.astype(jnp.float32))
        scores = scores + bias_heads + masked[None, None, :]
        top = lax.optimization_barrier(jnp.max(scores, axis=-1, keepdims=True))
        expo = jnp.exp(scores - top)
        total = lax.optimization_barrier(jnp.sum(expo, axis=-1))
        weights = expo.astype(jnp.bfloat16)
        attended = jnp.einsum('hjk,khd->jhd', weights.astype(jnp.float32), values.astype(jnp.float32))
        attended = attended / jnp.transpose(total)[:, :, None]
        gated = (attended.reshape(count, width) * jax.nn.sigmoid(gates.astype(jnp.float32))).astype(jnp.bfloat16)
        return jnp.dot(gated, w_out, preferred_element_type=jnp.float32).astype(jnp.bfloat16)
    return lax.map(one_row, pair)
```

```python
import functools

import jax
import jax.numpy as jnp
from jax import lax
from jax.experimental import pallas as pl
from jax.experimental.pallas import tpu as pltpu
from jax.sharding import PartitionSpec as P

F32 = jnp.float32
BF16 = jnp.bfloat16
VMEM = pl.BlockSpec(memory_space=pltpu.VMEM)
SMEM = pl.BlockSpec(memory_space=pltpu.SMEM)

SPLIT = 4
MASK_ROWS = 16


def norm_rows(values):
    center = jnp.mean(values, axis=-1, keepdims=True)
    shifted = values - center
    spread = jnp.mean(shifted * shifted, axis=-1, keepdims=True)
    return (shifted * lax.rsqrt(spread + 1e-05)).astype(BF16)


def pre_kernel(rows, cols, heads, pair_ref, w_bias_ref, normed_ref, spread_ref):
    normed = norm_rows(pair_ref[...].astype(F32))
    normed_ref[...] = normed
    width = normed.shape[1]
    lane = lax.broadcasted_iota(jnp.int32, (width, width), 1) // cols
    w_bias = w_bias_ref[...].astype(F32)
    wide = jnp.zeros((width, width), F32)
    for head in range(heads):
        wide = jnp.where(lane == head, w_bias[:, head : head + 1], wide)
    product = jnp.dot(normed, wide.astype(BF16), preferred_element_type=F32)
    column = lax.broadcasted_iota(jnp.int32, product.shape, 0) % cols
    place = lax.broadcasted_iota(jnp.int32, product.shape, 1) % cols
    product = jnp.where(column == place, product, 0.0)
    bias = jnp.sum(product.reshape(rows, cols, width), axis=1).astype(BF16)
    for member in range(spread_ref.shape[0]):
        spread_ref[member] = bias


def pack_kernel(normed_ref, bias_ref, mask_ref, send_ref):
    members = send_ref.shape[0]
    width = normed_ref.shape[1]
    part = normed_ref.shape[0] // SPLIT
    blocks = bias_ref.shape[0] // SPLIT
    depth = blocks * bias_ref.shape[1]
    for member in range(members):
        query_block, sub = divmod(member, SPLIT)
        send_ref[member, 0:part] = normed_ref[sub * part : (sub + 1) * part]
        chosen = bias_ref[query_block * blocks : (query_block + 1) * blocks]
        send_ref[member, part : part + depth] = chosen.reshape(depth, width)
        send_ref[member, part + depth :] = mask_ref[...]


def attend_kernel(
    heads, ids_ref, block_ref, other_ref, w_proj_ref, w_out_ref, out_ref, bias_ref, scores_ref
):
    members, _, width = block_ref.shape
    own_rows, cols = out_ref.shape[1], out_ref.shape[2]
    part = own_rows * cols
    depth = other_ref.shape[1]
    keys_count = members * cols
    queries = SPLIT * cols
    head_size = width // heads
    lanes = members * width
    first = ids_ref[0]
    parity = ids_ref[1]

    for member in range(members):
        mask = block_ref[member, part + depth :].astype(F32)[0:1]
        masked = (mask - 1.0) * 1e9
        own = block_ref[member, part : part + depth].astype(F32) + masked
        other = other_ref[member].astype(F32) + masked
        bias_ref[member, :, parity] = own.reshape(SPLIT, depth // SPLIT, width)
        bias_ref[member, :, 1 - parity] = other.reshape(SPLIT, depth // SPLIT, width)

    shape = (heads, cols, width)
    head_of_row = lax.broadcasted_iota(jnp.int32, shape, 0)
    head_of_lane = lax.broadcasted_iota(jnp.int32, shape, 2) // head_size
    same = (head_of_row == head_of_lane).astype(F32).astype(BF16)
    ones = jnp.broadcast_to(same[None], (members,) + shape).reshape(lanes, width)
    lane_head = lax.broadcasted_iota(jnp.int32, (queries, width), 1) // cols

    def spread(values):
        wide = values.reshape(members, 1, cols, width) * same[None]
        return wide.reshape(lanes, width)

    for row in range(own_rows):
        entries = block_ref[:, row * cols : (row + 1) * cols].reshape(keys_count, width)
        asking = block_ref[pl.ds(first, SPLIT), row * cols : (row + 1) * cols]
        asking = asking.reshape(queries, width)
        query = jnp.dot(asking, w_proj_ref[:, :width], preferred_element_type=F32)
        query = (query * head_size ** (-0.5)).astype(BF16)
        gates = jnp.dot(asking, w_proj_ref[:, 3 * width :], preferred_element_type=F32)
        gates = gates.astype(BF16).astype(F32)
        both = jnp.dot(entries, w_proj_ref[:, width : 3 * width], preferred_element_type=F32)
        both = both.astype(BF16)
        keys = spread(both[:, :width])
        values = jnp.concatenate([spread(both[:, width:]), ones], axis=1)

        scores = lax.dot_general(
            query, keys, (((1,), (1,)), ((), ())), preferred_element_type=F32
        )
        largest = None
        for member in range(members):
            piece = scores[:, member * width : (member + 1) * width]
            piece = piece + bias_ref[member].reshape(queries, width)
            scores_ref[row % 2, :, member * width : (member + 1) * width] = piece
            largest = piece if largest is None else jnp.maximum(largest, piece)
        top = jnp.zeros((queries, width), F32)
        for head in range(heads):
            chosen = jnp.where(lane_head == head, largest, -jnp.inf)
            top = jnp.where(lane_head == head, jnp.max(chosen, axis=-1, keepdims=True), top)
        pieces = []
        for member in range(members):
            piece = scores_ref[row % 2, :, member * width : (member + 1) * width]
            pieces.append(jnp.exp(piece - top).astype(BF16))
        weights = jnp.concatenate(pieces, axis=1)
        sums = jnp.dot(weights, values, preferred_element_type=F32)
        attended = sums[:, :width] / sums[:, width:]
        gated = (attended * jax.nn.sigmoid(gates)).astype(BF16)
        result = jnp.dot(gated, w_out_ref[...], preferred_element_type=F32).astype(BF16)
        out_ref[:, row] = result.reshape(SPLIT, cols, width)


def on_device(pair, w_proj, w_bias, w_out, token_mask, *, row_size, col_size):
    rows, cols, width = pair.shape
    heads = w_bias.shape[1]
    own_rows = rows // SPLIT
    half = row_size // 2
    queries = SPLIT * cols
    depth = queries // 2
    part = own_rows * cols
    chunk = part + depth + MASK_ROWS

    normed, spread = pl.pallas_call(
        functools.partial(pre_kernel, rows, cols, heads),
        out_shape=(
            jax.ShapeDtypeStruct((rows * cols, width), BF16),
            jax.ShapeDtypeStruct((half, rows, width), BF16),
        ),
        in_specs=[VMEM, VMEM],
        out_specs=(VMEM, VMEM),
    )(pair.reshape(rows * cols, width), w_bias)

    same_core = [[2 * n + core for n in range(half)] for core in range(2)]
    bias = lax.all_to_all(spread, "row", 0, 0, axis_index_groups=same_core, tiled=True)

    mask = jnp.tile(token_mask, width // cols).astype(BF16)
    mask = jnp.broadcast_to(mask[None], (MASK_ROWS, width))
    send = pl.pallas_call(
        pack_kernel,
        out_shape=jax.ShapeDtypeStruct((col_size, chunk, width), BF16),
        in_specs=[VMEM, VMEM, VMEM],
        out_specs=VMEM,
    )(normed, bias, mask)
    block = lax.all_to_all(send, "col", 0, 0, tiled=True)

    swap = [(r, r ^ 1) for r in range(row_size)]
    other = lax.ppermute(block[:, part : part + depth], "row", swap)

    ids = jnp.stack([lax.axis_index("col") // SPLIT * SPLIT, lax.axis_index("row") % 2])
    answer = pl.pallas_call(
        functools.partial(attend_kernel, heads),
        out_shape=jax.ShapeDtypeStruct((SPLIT, own_rows, cols, width), BF16),
        in_specs=[SMEM, VMEM, VMEM, VMEM, VMEM],
        out_specs=VMEM,
        scratch_shapes=[
            pltpu.VMEM((col_size, SPLIT, 2, depth // SPLIT, width), F32),
            pltpu.VMEM((2, queries, col_size * width), F32),
        ],
        compiler_params=pltpu.CompilerParams(vmem_limit_bytes=40 * 1024 * 1024),
    )(ids.astype(jnp.int32), block, other, w_proj, w_out)

    near = [[SPLIT * g + m for m in range(SPLIT)] for g in range(col_size // SPLIT)]
    back = lax.all_to_all(answer, "col", 0, 0, axis_index_groups=near, tiled=True)
    return back.reshape(rows, cols, width)


def solution(mesh):
    in_specs = (P("row", "col", None), P(), P(), P(), P("col"))
    out_specs = P("row", "col", None)
    body = functools.partial(on_device, row_size=mesh.shape["row"], col_size=mesh.shape["col"])
    return jax.shard_map(body, mesh=mesh, in_specs=in_specs, out_specs=out_specs, check_vma=False)
```

```python
import functools

import jax
import jax.numpy as jnp
from jax import lax
from jax.experimental import pallas as pl
from jax.experimental.pallas import tpu as pltpu
from jax.sharding import PartitionSpec as P

F32 = jnp.float32
BF16 = jnp.bfloat16
VMEM = pl.BlockSpec(memory_space=pltpu.VMEM)
ANY = pl.BlockSpec(memory_space=pl.ANY)

SPLIT = 4
CORES = 2


def norm_rows(values):
    center = jnp.mean(values, axis=-1, keepdims=True)
    shifted = values - center
    spread = jnp.mean(shifted * shifted, axis=-1, keepdims=True)
    return (shifted * lax.rsqrt(spread + 1e-05)).astype(BF16)


def norm_kernel(rows, cols, pair_ref, w_bias_ref, mask_ref, send_ref, spread_ref):
    normed = norm_rows(pair_ref[...].astype(F32))
    width = normed.shape[1]
    part = normed.shape[0] // SPLIT
    for member in range(send_ref.shape[0]):
        sub = member % SPLIT
        send_ref[member, 0:part] = normed[sub * part : (sub + 1) * part]

    heads = w_bias_ref.shape[0]
    head_of_row = lax.broadcasted_iota(jnp.int32, (width, width), 0) // cols
    w_bias = w_bias_ref[...].astype(F32)
    wide = jnp.zeros((width, width), F32)
    for head in range(heads):
        wide = jnp.where(head_of_row == head, w_bias[head : head + 1], wide)
    product = lax.dot_general(
        normed, wide.astype(BF16), (((1,), (1,)), ((), ())), preferred_element_type=F32
    )
    column = lax.broadcasted_iota(jnp.int32, product.shape, 0) % cols
    place = lax.broadcasted_iota(jnp.int32, product.shape, 1) % cols
    product = jnp.where(column == place, product, 0.0)
    bias = jnp.sum(product.reshape(rows, cols, width), axis=1).astype(BF16)
    masked = (mask_ref[...].astype(F32) - 1.0) * 1e9
    masked = jnp.concatenate([masked] * heads, axis=1)
    bias = (bias.astype(F32) + masked).astype(BF16)
    for member in range(spread_ref.shape[0]):
        spread_ref[member] = bias


def pack_kernel(bias_ref, half_ref, send_ref, done):
    del half_ref
    members, chunk, _ = send_ref.shape
    depth = bias_ref.shape[1]
    copies = [
        pltpu.make_async_copy(
            bias_ref.at[member // SPLIT],
            send_ref.at[member, pl.ds(chunk - depth, depth)],
            done.at[member],
        )
        for member in range(members)
    ]
    for copy in copies:
        copy.start()
    for copy in copies:
        copy.wait()


def project_kernel(heads, cols, own_rows, block_ref, w_proj_ref, w_out_ref, made_ref):
    members, _, width = block_ref.shape
    head_size = width // heads
    keys_count = members * cols
    queries = SPLIT * cols
    first = lax.axis_index("col") // SPLIT * SPLIT
    for row in range(own_rows):
        entries = block_ref[:, row * cols : (row + 1) * cols].reshape(keys_count, width)
        made_ref[row, :keys_count] = jnp.dot(
            entries, w_proj_ref[:, width : 3 * width], preferred_element_type=F32
        ).astype(BF16)
        asking = block_ref[pl.ds(first, SPLIT), row * cols : (row + 1) * cols]
        asking = asking.reshape(queries, width)
        query = jnp.dot(asking, w_proj_ref[:, :width], preferred_element_type=F32)
        made_ref[row, keys_count:, :width] = (query * head_size ** (-0.5)).astype(BF16)
        gates = jnp.dot(asking, w_proj_ref[:, 3 * width :], preferred_element_type=F32)
        made_ref[row, keys_count:, width:] = gates.astype(BF16)
    made_ref[own_rows, :width, :width] = w_out_ref[...]


def attend_kernel(heads, cols, block_ref, other_ref, made_ref, out_ref, bias_ref):
    members, depth, width = other_ref.shape
    own_rows = made_ref.shape[0] - 1
    queries = SPLIT * cols
    keys_count = members * cols
    group = width // cols
    part = block_ref.shape[1] - depth
    parity = lax.axis_index("row") % CORES

    segment = lax.broadcasted_iota(jnp.int32, (1, width), 1) // cols
    for turn in range(members // group):
        for source in range(CORES):
            turned = []
            for piece in range(group):
                member = turn * group + piece
                value = other_ref[member] if source else block_ref[member, part:]
                value = value.astype(F32)
                turned.append([value] + [pltpu.roll(value, cols * d, 1) for d in range(1, group)])
            core = 1 - parity if source else parity
            for head in range(heads):
                value = turned[0][-head % group]
                for piece in range(1, group):
                    value = jnp.where(segment == piece, turned[piece][(piece - head) % group], value)
                value = value.reshape(SPLIT, depth // SPLIT, width)
                bias_ref[head, :, core, :, turn * width : (turn + 1) * width] = value

    lane_head = lax.broadcasted_iota(jnp.int32, (1, width), 1) // (width // heads)
    w_out = made_ref[own_rows, :width, :width]
    ones = jnp.ones((keys_count, width), BF16)
    for row in range(own_rows):
        query = made_ref[row, keys_count:, :width].astype(F32)
        values = jnp.concatenate([made_ref[row, :keys_count, width:], ones], axis=1)
        above = jnp.zeros((queries, width), F32)
        below = jnp.zeros((queries, width), F32)
        for head in range(heads):
            chosen = jnp.where(lane_head == head, query, 0.0).astype(BF16)
            scores = lax.dot_general(
                chosen,
                made_ref[row, :keys_count, :width],
                (((1,), (1,)), ((), ())),
                preferred_element_type=F32,
            )
            scores = scores + bias_ref[head].reshape(queries, keys_count)
            top = jnp.max(scores, axis=-1, keepdims=True)
            weights = jnp.exp(scores - top).astype(BF16)
            sums = jnp.dot(weights, values, preferred_element_type=F32)
            above = jnp.where(lane_head == head, sums[:, :width], above)
            below = jnp.where(lane_head == head, sums[:, width:], below)
        gates = made_ref[row, keys_count:, width:].astype(F32)
        gated = (above / below * jax.nn.sigmoid(gates)).astype(BF16)
        result = jnp.dot(gated, w_out, preferred_element_type=F32).astype(BF16)
        out_ref[:, row] = result.reshape(SPLIT, cols, width)


def on_device(pair, w_proj, w_bias, w_out, token_mask, *, row_size, col_size):
    rows, cols, width = pair.shape
    heads = w_bias.shape[1]
    own_rows = rows // SPLIT
    half = row_size // CORES
    queries = SPLIT * cols
    keys_count = col_size * cols
    depth = queries // CORES
    part = own_rows * cols

    send, spread = pl.pallas_call(
        functools.partial(norm_kernel, rows, cols),
        out_shape=(
            jax.ShapeDtypeStruct((col_size, part + depth, width), BF16),
            jax.ShapeDtypeStruct((half, rows, width), BF16),
        ),
        in_specs=[VMEM, VMEM, VMEM],
        out_specs=(VMEM, VMEM),
    )(pair.reshape(rows * cols, width), w_bias.T, token_mask[None])

    same_core = [[CORES * n + core for n in range(half)] for core in range(CORES)]
    bias = lax.all_to_all(spread, "row", 0, 0, axis_index_groups=same_core, tiled=True)

    send = pl.pallas_call(
        pack_kernel,
        out_shape=jax.ShapeDtypeStruct(send.shape, BF16),
        in_specs=[VMEM, ANY],
        out_specs=ANY,
        scratch_shapes=[pltpu.SemaphoreType.DMA((col_size,))],
        input_output_aliases={1: 0},
    )(bias.reshape(SPLIT, depth, width), send)
    block = lax.all_to_all(send, "col", 0, 0, tiled=True)

    swap = [(r, r ^ 1) for r in range(row_size)]
    other = lax.ppermute(block[:, part:], "row", swap)

    made = pl.pallas_call(
        functools.partial(project_kernel, heads, cols, own_rows),
        out_shape=jax.ShapeDtypeStruct((own_rows + 1, keys_count + queries, 2 * width), BF16),
        in_specs=[VMEM, VMEM, VMEM],
        out_specs=VMEM,
        compiler_params=pltpu.CompilerParams(vmem_limit_bytes=16 << 20),
    )(block, w_proj, w_out)

    answer = pl.pallas_call(
        functools.partial(attend_kernel, heads, cols),
        out_shape=jax.ShapeDtypeStruct((SPLIT, own_rows, cols, width), BF16),
        in_specs=[VMEM, VMEM, VMEM],
        out_specs=VMEM,
        scratch_shapes=[pltpu.VMEM((heads, SPLIT, CORES, depth // SPLIT, keys_count), F32)],
        compiler_params=pltpu.CompilerParams(vmem_limit_bytes=16 << 20),
    )(block, other, made)

    near = [[SPLIT * g + m for m in range(SPLIT)] for g in range(col_size // SPLIT)]
    back = lax.all_to_all(answer, "col", 0, 0, axis_index_groups=near, tiled=True)
    return back.reshape(rows, cols, width)


def solution(mesh):
    in_specs = (P("row", "col", None), P(), P(), P(), P("col"))
    out_specs = P("row", "col", None)
    body = functools.partial(on_device, row_size=mesh.shape["row"], col_size=mesh.shape["col"])
    return jax.shard_map(body, mesh=mesh, in_specs=in_specs, out_specs=out_specs, check_vma=False)
```

```python
import functools

import jax
import jax.numpy as jnp
from jax import lax
from jax.experimental import pallas as pl
from jax.experimental.pallas import tpu as pltpu
from jax.sharding import PartitionSpec as P

F32 = jnp.float32
BF16 = jnp.bfloat16
VMEM = pl.BlockSpec(memory_space=pltpu.VMEM)
ANY = pl.BlockSpec(memory_space=pl.ANY)

SPLIT = 4
CORES = 2


def joined(group, sub):
    return sub // 2 * 2 * SPLIT + group * 2 + sub % 2


def sub_of(col):
    return col // (2 * SPLIT) * 2 + col % 2


def norm_rows(values):
    center = jnp.mean(values, axis=-1, keepdims=True)
    shifted = values - center
    spread = jnp.mean(shifted * shifted, axis=-1, keepdims=True)
    return (shifted * lax.rsqrt(spread + 1e-05)).astype(BF16)


def norm_kernel(rows, cols, pair_ref, w_bias_ref, mask_ref, send_ref, spread_ref):
    normed = norm_rows(pair_ref[...].astype(F32))
    width = normed.shape[1]
    part = normed.shape[0] // SPLIT
    for member in range(send_ref.shape[0]):
        sub = sub_of(member)
        send_ref[member, 0:part] = normed[sub * part : (sub + 1) * part]

    heads = w_bias_ref.shape[0]
    head_of_row = lax.broadcasted_iota(jnp.int32, (width, width), 0) // cols
    w_bias = w_bias_ref[...].astype(F32)
    wide = jnp.zeros((width, width), F32)
    for head in range(heads):
        wide = jnp.where(head_of_row == head, w_bias[head : head + 1], wide)
    product = lax.dot_general(
        normed, wide.astype(BF16), (((1,), (1,)), ((), ())), preferred_element_type=F32
    )
    column = lax.broadcasted_iota(jnp.int32, product.shape, 0) % cols
    place = lax.broadcasted_iota(jnp.int32, product.shape, 1) % cols
    product = jnp.where(column == place, product, 0.0)
    bias = jnp.sum(product.reshape(rows, cols, width), axis=1).astype(BF16)
    masked = (mask_ref[...].astype(F32) - 1.0) * 1e9
    masked = jnp.concatenate([masked] * heads, axis=1)
    bias = (bias.astype(F32) + masked).astype(BF16)
    for member in range(spread_ref.shape[0]):
        spread_ref[member] = bias


def project_kernel(heads, cols, own_rows, block_ref, w_proj_ref, w_out_ref, made_ref):
    members, _, width = block_ref.shape
    head_size = width // heads
    keys_count = members * cols
    queries = SPLIT * cols
    first = lax.axis_index("col") // 2 % SPLIT * 2
    for row in range(own_rows):
        entries = block_ref[:, row * cols : (row + 1) * cols].reshape(keys_count, width)
        made_ref[row, :keys_count] = jnp.dot(
            entries, w_proj_ref[:, width : 3 * width], preferred_element_type=F32
        ).astype(BF16)
        asking = [
            block_ref[pl.ds(first + start, 2), row * cols : (row + 1) * cols]
            for start in (0, 2 * SPLIT)
        ]
        asking = jnp.concatenate(asking, axis=0).reshape(queries, width)
        query = jnp.dot(asking, w_proj_ref[:, :width], preferred_element_type=F32)
        made_ref[row, keys_count:, :width] = (query * head_size ** (-0.5)).astype(BF16)
        gates = jnp.dot(asking, w_proj_ref[:, 3 * width :], preferred_element_type=F32)
        made_ref[row, keys_count:, width:] = gates.astype(BF16)
    made_ref[own_rows, :width, :width] = w_out_ref[...]


def attend_kernel(heads, cols, block_ref, other_ref, made_ref, out_ref, bias_ref):
    members, depth, width = other_ref.shape
    own_rows = made_ref.shape[0] - 1
    queries = SPLIT * cols
    keys_count = members * cols
    group = width // cols
    part = block_ref.shape[1] - depth
    parity = lax.axis_index("row") % CORES

    segment = lax.broadcasted_iota(jnp.int32, (1, width), 1) // cols
    for turn in range(members // group):
        for source in range(CORES):
            turned = []
            for piece in range(group):
                member = turn * group + piece
                value = other_ref[member] if source else block_ref[member, part:]
                value = value.astype(F32)
                turned.append([value] + [pltpu.roll(value, cols * d, 1) for d in range(1, group)])
            core = 1 - parity if source else parity
            for head in range(heads):
                value = turned[0][-head % group]
                for piece in range(1, group):
                    value = jnp.where(segment == piece, turned[piece][(piece - head) % group], value)
                value = value.reshape(SPLIT, depth // SPLIT, width)
                bias_ref[head, :, core, :, turn * width : (turn + 1) * width] = value

    lane_head = lax.broadcasted_iota(jnp.int32, (1, width), 1) // (width // heads)
    w_out = made_ref[own_rows, :width, :width]
    ones = jnp.ones((keys_count, width), BF16)
    for row in range(own_rows):
        query = made_ref[row, keys_count:, :width].astype(F32)
        values = jnp.concatenate([made_ref[row, :keys_count, width:], ones], axis=1)
        above = jnp.zeros((queries, width), F32)
        below = jnp.zeros((queries, width), F32)
        for head in range(heads):
            chosen = jnp.where(lane_head == head, query, 0.0).astype(BF16)
            scores = lax.dot_general(
                chosen,
                made_ref[row, :keys_count, :width],
                (((1,), (1,)), ((), ())),
                preferred_element_type=F32,
            )
            scores = scores + bias_ref[head].reshape(queries, keys_count)
            top = jnp.max(scores, axis=-1, keepdims=True)
            weights = jnp.exp(scores - top).astype(BF16)
            sums = jnp.dot(weights, values, preferred_element_type=F32)
            above = jnp.where(lane_head == head, sums[:, :width], above)
            below = jnp.where(lane_head == head, sums[:, width:], below)
        gates = made_ref[row, keys_count:, width:].astype(F32)
        gated = (above / below * jax.nn.sigmoid(gates)).astype(BF16)
        result = jnp.dot(gated, w_out, preferred_element_type=F32).astype(BF16)
        out_ref[:, row] = result.reshape(SPLIT, cols, width)


def on_device(pair, w_proj, w_bias, w_out, token_mask, *, row_size, col_size):
    rows, cols, width = pair.shape
    heads = w_bias.shape[1]
    own_rows = rows // SPLIT
    half = row_size // CORES
    queries = SPLIT * cols
    keys_count = col_size * cols
    depth = queries // CORES
    part = own_rows * cols

    send, spread = pl.pallas_call(
        functools.partial(norm_kernel, rows, cols),
        out_shape=(
            jax.ShapeDtypeStruct((col_size, part + depth, width), BF16),
            jax.ShapeDtypeStruct((half, rows, width), BF16),
        ),
        in_specs=[VMEM, VMEM, VMEM],
        out_specs=(VMEM, VMEM),
    )(pair.reshape(rows * cols, width), w_bias.T, token_mask[None])

    same_core = [[CORES * n + core for n in range(half)] for core in range(CORES)]
    bias = lax.all_to_all(spread, "row", 0, 0, axis_index_groups=same_core, tiled=True)

    bias = bias.reshape(2, SPLIT, 2, rows, width).transpose(1, 0, 2, 3, 4).reshape(SPLIT, 1, depth, width)
    bias = jnp.broadcast_to(bias[None], (2, SPLIT, 2, depth, width)).reshape(col_size, depth, width)
    send = lax.dynamic_update_slice(send, bias, (0, part, 0))
    block = lax.all_to_all(send, "col", 0, 0, tiled=True)

    swap = [(r, r ^ 1) for r in range(row_size)]
    other = lax.ppermute(block[:, part:], "row", swap)

    made = pl.pallas_call(
        functools.partial(project_kernel, heads, cols, own_rows),
        out_shape=jax.ShapeDtypeStruct((own_rows + 1, keys_count + queries, 2 * width), BF16),
        in_specs=[VMEM, VMEM, VMEM],
        out_specs=VMEM,
        compiler_params=pltpu.CompilerParams(vmem_limit_bytes=16 << 20),
    )(block, w_proj, w_out)

    answer = pl.pallas_call(
        functools.partial(attend_kernel, heads, cols),
        out_shape=jax.ShapeDtypeStruct((SPLIT, own_rows, cols, width), BF16),
        in_specs=[VMEM, VMEM, VMEM],
        out_specs=VMEM,
        scratch_shapes=[pltpu.VMEM((heads, SPLIT, CORES, depth // SPLIT, keys_count), F32)],
        compiler_params=pltpu.CompilerParams(vmem_limit_bytes=16 << 20),
    )(block, other, made)

    near = [[joined(group, sub) for sub in range(SPLIT)] for group in range(SPLIT)]
    answer = answer.reshape(rows, cols, width)
    return lax.all_to_all(answer, "col", 0, 0, axis_index_groups=near, tiled=True)


def solution(mesh):
    in_specs = (P("row", "col", None), P(), P(), P(), P("col"))
    out_specs = P("row", "col", None)
    body = functools.partial(on_device, row_size=mesh.shape["row"], col_size=mesh.shape["col"])
    return jax.shard_map(body, mesh=mesh, in_specs=in_specs, out_specs=out_specs, check_vma=False)
```

```python
import functools

import jax
import jax.numpy as jnp
from jax import lax
from jax.experimental import pallas as pl
from jax.experimental.pallas import tpu as pltpu
from jax.sharding import PartitionSpec as P

F32 = jnp.float32
BF16 = jnp.bfloat16
VMEM = pl.BlockSpec(memory_space=pltpu.VMEM)

SPLIT = 4
CORES = 2


def joined(group, sub):
    return sub // 2 * 2 * SPLIT + group * 2 + sub % 2


def sub_of(col):
    return col // (2 * SPLIT) * 2 + col % 2


def norm_rows(values):
    center = jnp.mean(values, axis=-1, keepdims=True)
    shifted = values - center
    spread = jnp.mean(shifted * shifted, axis=-1, keepdims=True)
    return (shifted * lax.rsqrt(spread + 1e-05)).astype(BF16)


def norm_kernel(rows, cols, pair_ref, w_bias_ref, mask_ref, send_ref, spread_ref):
    normed = norm_rows(pair_ref[...].astype(F32))
    width = normed.shape[1]
    part = normed.shape[0] // SPLIT
    for member in range(send_ref.shape[0]):
        sub = sub_of(member)
        send_ref[member, 0:part] = normed[sub * part : (sub + 1) * part]

    heads = w_bias_ref.shape[0]
    head_of_row = lax.broadcasted_iota(jnp.int32, (width, width), 0) // cols
    w_bias = w_bias_ref[...].astype(F32)
    wide = jnp.zeros((width, width), F32)
    for head in range(heads):
        wide = jnp.where(head_of_row == head, w_bias[head : head + 1], wide)
    product = lax.dot_general(
        normed, wide.astype(BF16), (((1,), (1,)), ((), ())), preferred_element_type=F32
    )
    column = lax.broadcasted_iota(jnp.int32, product.shape, 0) % cols
    place = lax.broadcasted_iota(jnp.int32, product.shape, 1) % cols
    product = jnp.where(column == place, product, 0.0)
    bias = jnp.sum(product.reshape(rows, cols, width), axis=1).astype(BF16)
    masked = (mask_ref[...].astype(F32) - 1.0) * 1e9
    masked = jnp.concatenate([masked] * heads, axis=1)
    bias = (bias.astype(F32) + masked).astype(BF16)
    for member in range(spread_ref.shape[0]):
        spread_ref[member] = bias


def project_kernel(heads, cols, own_rows, block_ref, w_proj_ref, w_out_ref, made_ref):
    members, _, width = block_ref.shape
    head_size = width // heads
    keys_count = members * cols
    queries = SPLIT * cols
    first = lax.axis_index("col") // 2 % SPLIT * 2
    for row in range(own_rows):
        entries = block_ref[:, row * cols : (row + 1) * cols].reshape(keys_count, width)
        made_ref[row, :keys_count] = jnp.dot(
            entries, w_proj_ref[:, width : 3 * width], preferred_element_type=F32
        ).astype(BF16)
        asking = [
            block_ref[pl.ds(first + start, 2), row * cols : (row + 1) * cols]
            for start in (0, 2 * SPLIT)
        ]
        asking = jnp.concatenate(asking, axis=0).reshape(queries, width)
        query = jnp.dot(asking, w_proj_ref[:, :width], preferred_element_type=F32)
        made_ref[row, keys_count:, :width] = (query * head_size ** (-0.5)).astype(BF16)
        gates = jnp.dot(asking, w_proj_ref[:, 3 * width :], preferred_element_type=F32)
        made_ref[row, keys_count:, width:] = gates.astype(BF16)
    made_ref[own_rows, :width, :width] = w_out_ref[...]


def attend_kernel(heads, cols, block_ref, other_ref, made_ref, out_ref, bias_ref):
    members, depth, width = other_ref.shape
    own_rows = made_ref.shape[0] - 1
    queries = SPLIT * cols
    keys_count = members * cols
    group = width // cols
    part = block_ref.shape[1] - depth
    parity = lax.axis_index("row") % CORES

    lane_head = lax.broadcasted_iota(jnp.int32, (1, width), 1) // (width // heads)

    def products(row):
        query = made_ref[row, keys_count:, :width].astype(F32)
        wide = [jnp.where(lane_head == head, query, 0.0).astype(BF16) for head in range(heads)]
        return lax.dot_general(
            jnp.concatenate(wide, axis=0),
            made_ref[row, :keys_count, :width],
            (((1,), (1,)), ((), ())),
            preferred_element_type=F32,
        )

    ahead = products(0)
    segment = lax.broadcasted_iota(jnp.int32, (1, width), 1) // cols
    for turn in range(members // group):
        for source in range(CORES):
            turned = []
            for piece in range(group):
                member = turn * group + piece
                value = other_ref[member] if source else block_ref[member, part:]
                value = value.astype(F32)
                turned.append([value] + [pltpu.roll(value, cols * d, 1) for d in range(1, group)])
            core = 1 - parity if source else parity
            for head in range(heads):
                value = turned[0][-head % group]
                for piece in range(1, group):
                    value = jnp.where(segment == piece, turned[piece][(piece - head) % group], value)
                value = value.reshape(SPLIT, depth // SPLIT, width)
                bias_ref[head, :, core, :, turn * width : (turn + 1) * width] = value

    w_out = made_ref[own_rows, :width, :width]
    ones = jnp.ones((keys_count, width), BF16)
    gated = []
    for row in range(own_rows):
        scores = ahead
        if row + 1 < own_rows:
            ahead = products(row + 1)
        weights = []
        for head in range(heads):
            value = scores[head * queries : (head + 1) * queries]
            value = value + bias_ref[head].reshape(queries, keys_count)
            top = jnp.max(value, axis=-1, keepdims=True)
            weights.append(jnp.exp(value - top).astype(BF16))
        values = jnp.concatenate([made_ref[row, :keys_count, width:], ones], axis=1)
        above = jnp.zeros((queries, width), F32)
        below = jnp.zeros((queries, width), F32)
        for head in range(heads):
            sums = jnp.dot(weights[head], values, preferred_element_type=F32)
            above = jnp.where(lane_head == head, sums[:, :width], above)
            below = jnp.where(lane_head == head, sums[:, width:], below)
        gates = made_ref[row, keys_count:, width:].astype(F32)
        gated.append((above / below * jax.nn.sigmoid(gates)).astype(BF16))
    result = jnp.dot(jnp.concatenate(gated, axis=0), w_out, preferred_element_type=F32).astype(BF16)
    for row in range(own_rows):
        out_ref[:, row] = result[row * queries : (row + 1) * queries].reshape(SPLIT, cols, width)


def on_device(pair, w_proj, w_bias, w_out, token_mask, *, row_size, col_size):
    rows, cols, width = pair.shape
    heads = w_bias.shape[1]
    own_rows = rows // SPLIT
    half = row_size // CORES
    queries = SPLIT * cols
    keys_count = col_size * cols
    depth = queries // CORES
    part = own_rows * cols

    send, spread = pl.pallas_call(
        functools.partial(norm_kernel, rows, cols),
        out_shape=(
            jax.ShapeDtypeStruct((col_size, part + depth, width), BF16),
            jax.ShapeDtypeStruct((half, rows, width), BF16),
        ),
        in_specs=[VMEM, VMEM, VMEM],
        out_specs=(VMEM, VMEM),
    )(pair.reshape(rows * cols, width), w_bias.T, token_mask[None])

    same_core = [[CORES * n + core for n in range(half)] for core in range(CORES)]
    bias = lax.all_to_all(spread, "row", 0, 0, axis_index_groups=same_core, tiled=True)

    bias = bias.reshape(2, SPLIT, 2, rows, width).transpose(1, 0, 2, 3, 4).reshape(SPLIT, 1, depth, width)
    bias = jnp.broadcast_to(bias[None], (2, SPLIT, 2, depth, width)).reshape(col_size, depth, width)
    send = lax.dynamic_update_slice(send, bias, (0, part, 0))
    block = lax.all_to_all(send, "col", 0, 0, tiled=True)

    swap = [(r, r ^ 1) for r in range(row_size)]
    other = lax.ppermute(block[:, part:], "row", swap)

    made = pl.pallas_call(
        functools.partial(project_kernel, heads, cols, own_rows),
        out_shape=jax.ShapeDtypeStruct((own_rows + 1, keys_count + queries, 2 * width), BF16),
        in_specs=[VMEM, VMEM, VMEM],
        out_specs=VMEM,
        compiler_params=pltpu.CompilerParams(vmem_limit_bytes=16 << 20),
    )(block, w_proj, w_out)

    answer = pl.pallas_call(
        functools.partial(attend_kernel, heads, cols),
        out_shape=jax.ShapeDtypeStruct((SPLIT, own_rows, cols, width), BF16),
        in_specs=[VMEM, VMEM, VMEM],
        out_specs=VMEM,
        scratch_shapes=[pltpu.VMEM((heads, SPLIT, CORES, depth // SPLIT, keys_count), F32)],
        compiler_params=pltpu.CompilerParams(vmem_limit_bytes=16 << 20),
    )(block, other, made)

    near = [[joined(group, sub) for sub in range(SPLIT)] for group in range(SPLIT)]
    answer = answer.reshape(rows, cols, width)
    return lax.all_to_all(answer, "col", 0, 0, axis_index_groups=near, tiled=True)


def solution(mesh):
    in_specs = (P("row", "col", None), P(), P(), P(), P("col"))
    out_specs = P("row", "col", None)
    body = functools.partial(on_device, row_size=mesh.shape["row"], col_size=mesh.shape["col"])
    return jax.shard_map(body, mesh=mesh, in_specs=in_specs, out_specs=out_specs, check_vma=False)
```

```python
import functools

import jax
import jax.numpy as jnp
from jax import lax
from jax.experimental import pallas as pl
from jax.experimental.pallas import tpu as pltpu
from jax.sharding import PartitionSpec as P

F32 = jnp.float32
BF16 = jnp.bfloat16
VMEM = pl.BlockSpec(memory_space=pltpu.VMEM)

SPLIT = 4
CORES = 2


def joined(group, sub):
    return sub // 2 * 2 * SPLIT + group * 2 + sub % 2


def sub_of(col):
    return col // (2 * SPLIT) * 2 + col % 2


def norm_rows(values):
    center = jnp.mean(values, axis=-1, keepdims=True)
    shifted = values - center
    spread = jnp.mean(shifted * shifted, axis=-1, keepdims=True)
    return (shifted * lax.rsqrt(spread + 1e-05)).astype(BF16)


def norm_kernel(pair_ref, send_ref, normed_ref):
    normed = norm_rows(pair_ref[...].astype(F32))
    normed_ref[...] = normed
    part = normed.shape[0] // SPLIT
    for member in range(send_ref.shape[0]):
        sub = sub_of(member)
        send_ref[member, 0:part] = normed[sub * part : (sub + 1) * part]


def bias_kernel(rows, cols, normed_ref, w_bias_ref, mask_ref, spread_ref):
    heads, width = w_bias_ref.shape
    head_of_row = lax.broadcasted_iota(jnp.int32, (width, width), 0) // cols
    w_bias = w_bias_ref[...].astype(F32)
    wide = jnp.zeros((width, width), F32)
    for head in range(heads):
        wide = jnp.where(head_of_row == head, w_bias[head : head + 1], wide)
    product = lax.dot_general(
        normed_ref[...], wide.astype(BF16), (((1,), (1,)), ((), ())), preferred_element_type=F32
    )
    column = lax.broadcasted_iota(jnp.int32, product.shape, 0) % cols
    place = lax.broadcasted_iota(jnp.int32, product.shape, 1) % cols
    product = jnp.where(column == place, product, 0.0)
    bias = jnp.sum(product.reshape(rows, cols, width), axis=1).astype(BF16)
    masked = (mask_ref[...].astype(F32) - 1.0) * 1e9
    masked = jnp.concatenate([masked] * heads, axis=1)
    bias = (bias.astype(F32) + masked).astype(BF16)
    for member in range(spread_ref.shape[0]):
        spread_ref[member] = bias


def products(heads, keys_count, made_ref, row):
    width = made_ref.shape[2] // 2
    lane_head = lax.broadcasted_iota(jnp.int32, (1, width), 1) // (width // heads)
    query = made_ref[row, keys_count:, :width].astype(F32)
    wide = [jnp.where(lane_head == head, query, 0.0).astype(BF16) for head in range(heads)]
    return lax.dot_general(
        jnp.concatenate(wide, axis=0),
        made_ref[row, :keys_count, :width],
        (((1,), (1,)), ((), ())),
        preferred_element_type=F32,
    )


def project_kernel(heads, cols, own_rows, block_ref, w_proj_ref, w_out_ref, made_ref, ahead_ref):
    members, _, width = block_ref.shape
    head_size = width // heads
    keys_count = members * cols
    queries = SPLIT * cols
    first = lax.axis_index("col") // 2 % SPLIT * 2
    for row in range(own_rows):
        entries = block_ref[:, row * cols : (row + 1) * cols].reshape(keys_count, width)
        made_ref[row, :keys_count] = jnp.dot(
            entries, w_proj_ref[:, width : 3 * width], preferred_element_type=F32
        ).astype(BF16)
        asking = [
            block_ref[pl.ds(first + start, 2), row * cols : (row + 1) * cols]
            for start in (0, 2 * SPLIT)
        ]
        asking = jnp.concatenate(asking, axis=0).reshape(queries, width)
        query = jnp.dot(asking, w_proj_ref[:, :width], preferred_element_type=F32)
        made_ref[row, keys_count:, :width] = (query * head_size ** (-0.5)).astype(BF16)
        gates = jnp.dot(asking, w_proj_ref[:, 3 * width :], preferred_element_type=F32)
        made_ref[row, keys_count:, width:] = gates.astype(BF16)
    made_ref[own_rows, :width, :width] = w_out_ref[...]
    ahead_ref[...] = products(heads, keys_count, made_ref, 0)


def attend_kernel(heads, cols, block_ref, other_ref, made_ref, ahead_ref, out_ref, bias_ref):
    members, depth, width = other_ref.shape
    own_rows = made_ref.shape[0] - 1
    queries = SPLIT * cols
    keys_count = members * cols
    group = width // cols
    part = block_ref.shape[1] - depth
    parity = lax.axis_index("row") % CORES

    lane_head = lax.broadcasted_iota(jnp.int32, (1, width), 1) // (width // heads)

    segment = lax.broadcasted_iota(jnp.int32, (1, width), 1) // cols
    for turn in range(members // group):
        for source in range(CORES):
            turned = []
            for piece in range(group):
                member = turn * group + piece
                value = other_ref[member] if source else block_ref[member, part:]
                value = value.astype(F32)
                turned.append([value] + [pltpu.roll(value, cols * d, 1) for d in range(1, group)])
            core = 1 - parity if source else parity
            for head in range(heads):
                value = turned[0][-head % group]
                for piece in range(1, group):
                    value = jnp.where(segment == piece, turned[piece][(piece - head) % group], value)
                value = value.reshape(SPLIT, depth // SPLIT, width)
                bias_ref[head, :, core, :, turn * width : (turn + 1) * width] = value

    w_out = made_ref[own_rows, :width, :width]
    ones = jnp.ones((keys_count, width), BF16)
    gated = []
    for row in range(own_rows):
        scores = ahead_ref if row == 0 else ahead
        if row + 1 < own_rows:
            ahead = products(heads, keys_count, made_ref, row + 1)
        weights = []
        for head in range(heads):
            value = scores[head * queries : (head + 1) * queries]
            value = value + bias_ref[head].reshape(queries, keys_count)
            top = jnp.max(value, axis=-1, keepdims=True)
            weights.append(jnp.exp(value - top).astype(BF16))
        values = jnp.concatenate([made_ref[row, :keys_count, width:], ones], axis=1)
        above = jnp.zeros((queries, width), F32)
        below = jnp.zeros((queries, width), F32)
        for head in range(heads):
            sums = jnp.dot(weights[head], values, preferred_element_type=F32)
            above = jnp.where(lane_head == head, sums[:, :width], above)
            below = jnp.where(lane_head == head, sums[:, width:], below)
        gates = made_ref[row, keys_count:, width:].astype(F32)
        gated.append((above / below * jax.nn.sigmoid(gates)).astype(BF16))
    result = jnp.dot(jnp.concatenate(gated, axis=0), w_out, preferred_element_type=F32).astype(BF16)
    for row in range(own_rows):
        out_ref[:, row] = result[row * queries : (row + 1) * queries].reshape(SPLIT, cols, width)


def on_device(pair, w_proj, w_bias, w_out, token_mask, *, row_size, col_size):
    rows, cols, width = pair.shape
    heads = w_bias.shape[1]
    own_rows = rows // SPLIT
    half = row_size // CORES
    queries = SPLIT * cols
    keys_count = col_size * cols
    depth = queries // CORES
    part = own_rows * cols

    send, normed = pl.pallas_call(
        norm_kernel,
        out_shape=(
            jax.ShapeDtypeStruct((col_size, part + depth, width), BF16),
            jax.ShapeDtypeStruct((rows * cols, width), BF16),
        ),
        in_specs=[VMEM],
        out_specs=(VMEM, VMEM),
        compiler_params=pltpu.CompilerParams(vmem_limit_bytes=4 << 20),
        cost_estimate=pl.CostEstimate(flops=1 << 30, bytes_accessed=16 << 20, transcendentals=0),
    )(pair.reshape(rows * cols, width))
    spread = pl.pallas_call(
        functools.partial(bias_kernel, rows, cols),
        out_shape=jax.ShapeDtypeStruct((half, rows, width), BF16),
        in_specs=[VMEM, VMEM, VMEM],
        out_specs=VMEM,
        compiler_params=pltpu.CompilerParams(vmem_limit_bytes=4 << 20),
    )(normed, w_bias.T, token_mask[None])

    same_core = [
        [CORES * joined(group, sub) + core for group in range(SPLIT) for sub in range(SPLIT)]
        for core in range(CORES)
    ]
    bias = lax.all_to_all(spread, "row", 0, 0, axis_index_groups=same_core, tiled=True)

    bias = bias.reshape(1, SPLIT, 1, depth, width)
    bias = jnp.broadcast_to(bias, (2, SPLIT, 2, depth, width)).reshape(col_size, depth, width)
    send = lax.dynamic_update_slice(send, bias, (0, part, 0))
    block = lax.all_to_all(send, "col", 0, 0, tiled=True)

    swap = [(r, r ^ 1) for r in range(row_size)]
    other = lax.ppermute(block[:, part:], "row", swap)

    made, ahead = pl.pallas_call(
        functools.partial(project_kernel, heads, cols, own_rows),
        out_shape=(
            jax.ShapeDtypeStruct((own_rows + 1, keys_count + queries, 2 * width), BF16),
            jax.ShapeDtypeStruct((heads * queries, keys_count), F32),
        ),
        in_specs=[VMEM, VMEM, VMEM],
        out_specs=(VMEM, VMEM),
        compiler_params=pltpu.CompilerParams(vmem_limit_bytes=12 << 20),
    )(block, w_proj, w_out)

    answer = pl.pallas_call(
        functools.partial(attend_kernel, heads, cols),
        out_shape=jax.ShapeDtypeStruct((SPLIT, own_rows, cols, width), BF16),
        in_specs=[VMEM, VMEM, VMEM, VMEM],
        out_specs=VMEM,
        scratch_shapes=[pltpu.VMEM((heads, SPLIT, CORES, depth // SPLIT, keys_count), F32)],
        compiler_params=pltpu.CompilerParams(vmem_limit_bytes=12 << 20),
    )(block, other, made, ahead)

    near = [[joined(group, sub) for sub in range(SPLIT)] for group in range(SPLIT)]
    answer = answer.reshape(rows, cols, width)
    return lax.all_to_all(answer, "col", 0, 0, axis_index_groups=near, tiled=True)


def solution(mesh):
    in_specs = (P("row", "col", None), P(), P(), P(), P("col"))
    out_specs = P("row", "col", None)
    body = functools.partial(on_device, row_size=mesh.shape["row"], col_size=mesh.shape["col"])
    return jax.shard_map(body, mesh=mesh, in_specs=in_specs, out_specs=out_specs, check_vma=False)
```

```python
import functools

import jax
import jax.numpy as jnp
from jax import lax
from jax.experimental import pallas as pl
from jax.experimental.pallas import tpu as pltpu
from jax.sharding import PartitionSpec as P

F32 = jnp.float32
BF16 = jnp.bfloat16
VMEM = pl.BlockSpec(memory_space=pltpu.VMEM)
HBM = pl.BlockSpec(memory_space=pltpu.HBM)

SPLIT = 4
CORES = 2


def joined(group, sub):
    return sub // 2 * 2 * SPLIT + group * 2 + sub % 2


def sub_of(col):
    return col // (2 * SPLIT) * 2 + col % 2


def norm_rows(values):
    center = jnp.mean(values, axis=-1, keepdims=True)
    shifted = values - center
    spread = jnp.mean(shifted * shifted, axis=-1, keepdims=True)
    return (shifted * lax.rsqrt(spread + 1e-05)).astype(BF16)


def norm_kernel(
    rows, cols, pair_hbm, w_bias_hbm, mask_hbm, send_ref, spread_ref, pair_ref, w_bias_ref, mask_ref, read
):
    sources = (pair_hbm, w_bias_hbm, mask_hbm)
    targets = (pair_ref, w_bias_ref, mask_ref)
    copies = [
        pltpu.make_async_copy(source, target, read.at[place])
        for place, (source, target) in enumerate(zip(sources, targets))
    ]
    for copy in copies:
        copy.start()
    copies[0].wait()
    normed = norm_rows(pair_ref[...].astype(F32))
    part = normed.shape[0] // SPLIT
    for member in range(send_ref.shape[0]):
        sub = sub_of(member)
        send_ref[member, 0:part] = normed[sub * part : (sub + 1) * part]

    copies[1].wait()
    copies[2].wait()
    heads, width = w_bias_ref.shape
    head_of_row = lax.broadcasted_iota(jnp.int32, (width, width), 0) // cols
    w_bias = w_bias_ref[...].astype(F32)
    wide = jnp.zeros((width, width), F32)
    for head in range(heads):
        wide = jnp.where(head_of_row == head, w_bias[head : head + 1], wide)
    product = lax.dot_general(
        normed, wide.astype(BF16), (((1,), (1,)), ((), ())), preferred_element_type=F32
    )
    column = lax.broadcasted_iota(jnp.int32, product.shape, 0) % cols
    place = lax.broadcasted_iota(jnp.int32, product.shape, 1) % cols
    product = jnp.where(column == place, product, 0.0)
    bias = jnp.sum(product.reshape(rows, cols, width), axis=1).astype(BF16)
    masked = (mask_ref[...].astype(F32) - 1.0) * 1e9
    masked = jnp.concatenate([masked] * heads, axis=1)
    bias = (bias.astype(F32) + masked).astype(BF16)
    for member in range(spread_ref.shape[0]):
        spread_ref[member] = bias


def products(heads, keys_count, made_ref, row):
    width = made_ref.shape[2] // 2
    lane_head = lax.broadcasted_iota(jnp.int32, (1, width), 1) // (width // heads)
    query = made_ref[row, keys_count:, :width].astype(F32)
    wide = [jnp.where(lane_head == head, query, 0.0).astype(BF16) for head in range(heads)]
    return lax.dot_general(
        jnp.concatenate(wide, axis=0),
        made_ref[row, :keys_count, :width],
        (((1,), (1,)), ((), ())),
        preferred_element_type=F32,
    )


def project_kernel(heads, cols, own_rows, block_ref, w_proj_ref, w_out_ref, made_ref, ahead_ref):
    members, _, width = block_ref.shape
    head_size = width // heads
    keys_count = members * cols
    queries = SPLIT * cols
    first = lax.axis_index("col") // 2 % SPLIT * 2
    for row in range(own_rows):
        entries = block_ref[:, row * cols : (row + 1) * cols].reshape(keys_count, width)
        made_ref[row, :keys_count] = jnp.dot(
            entries, w_proj_ref[:, width : 3 * width], preferred_element_type=F32
        ).astype(BF16)
        asking = [
            block_ref[pl.ds(first + start, 2), row * cols : (row + 1) * cols]
            for start in (0, 2 * SPLIT)
        ]
        asking = jnp.concatenate(asking, axis=0).reshape(queries, width)
        query = jnp.dot(asking, w_proj_ref[:, :width], preferred_element_type=F32)
        made_ref[row, keys_count:, :width] = (query * head_size ** (-0.5)).astype(BF16)
        gates = jnp.dot(asking, w_proj_ref[:, 3 * width :], preferred_element_type=F32)
        made_ref[row, keys_count:, width:] = gates.astype(BF16)
    made_ref[own_rows, :width, :width] = w_out_ref[...]
    ahead_ref[...] = products(heads, keys_count, made_ref, 0)


def attend_kernel(heads, cols, block_ref, other_ref, made_ref, ahead_ref, out_ref, bias_ref):
    members, depth, width = other_ref.shape
    own_rows = made_ref.shape[0] - 1
    queries = SPLIT * cols
    keys_count = members * cols
    group = width // cols
    part = block_ref.shape[1] - depth
    parity = lax.axis_index("row") % CORES

    lane_head = lax.broadcasted_iota(jnp.int32, (1, width), 1) // (width // heads)

    segment = lax.broadcasted_iota(jnp.int32, (1, width), 1) // cols
    for turn in range(members // group):
        for source in range(CORES):
            turned = []
            for piece in range(group):
                member = turn * group + piece
                value = other_ref[member] if source else block_ref[member, part:]
                value = value.astype(F32)
                turned.append([value] + [pltpu.roll(value, cols * d, 1) for d in range(1, group)])
            core = 1 - parity if source else parity
            for head in range(heads):
                value = turned[0][-head % group]
                for piece in range(1, group):
                    value = jnp.where(segment == piece, turned[piece][(piece - head) % group], value)
                value = value.reshape(SPLIT, depth // SPLIT, width)
                bias_ref[head, :, core, :, turn * width : (turn + 1) * width] = value

    w_out = made_ref[own_rows, :width, :width]
    ones = jnp.ones((keys_count, width), BF16)
    gated = []
    for row in range(own_rows):
        scores = ahead_ref if row == 0 else ahead
        if row + 1 < own_rows:
            ahead = products(heads, keys_count, made_ref, row + 1)
        weights = []
        for head in range(heads):
            value = scores[head * queries : (head + 1) * queries]
            value = value + bias_ref[head].reshape(queries, keys_count)
            top = jnp.max(value, axis=-1, keepdims=True)
            weights.append(jnp.exp(value - top).astype(BF16))
        values = jnp.concatenate([made_ref[row, :keys_count, width:], ones], axis=1)
        above = jnp.zeros((queries, width), F32)
        below = jnp.zeros((queries, width), F32)
        for head in range(heads):
            sums = jnp.dot(weights[head], values, preferred_element_type=F32)
            above = jnp.where(lane_head == head, sums[:, :width], above)
            below = jnp.where(lane_head == head, sums[:, width:], below)
        gates = made_ref[row, keys_count:, width:].astype(F32)
        gated.append((above / below * jax.nn.sigmoid(gates)).astype(BF16))
    result = jnp.dot(jnp.concatenate(gated, axis=0), w_out, preferred_element_type=F32).astype(BF16)
    for row in range(own_rows):
        out_ref[:, row] = result[row * queries : (row + 1) * queries].reshape(SPLIT, cols, width)


def on_device(pair, w_proj, w_bias, w_out, token_mask, *, row_size, col_size):
    rows, cols, width = pair.shape
    heads = w_bias.shape[1]
    own_rows = rows // SPLIT
    half = row_size // CORES
    queries = SPLIT * cols
    keys_count = col_size * cols
    depth = queries // CORES
    part = own_rows * cols

    given = (pair.reshape(rows * cols, width), w_bias.T, token_mask[None])
    given = [pltpu.with_memory_space_constraint(array, pltpu.HBM) for array in given]
    send, spread = pl.pallas_call(
        functools.partial(norm_kernel, rows, cols),
        out_shape=(
            jax.ShapeDtypeStruct((col_size, part + depth, width), BF16),
            jax.ShapeDtypeStruct((half, rows, width), BF16),
        ),
        in_specs=[HBM, HBM, HBM],
        out_specs=(VMEM, VMEM),
        scratch_shapes=[
            pltpu.VMEM((rows * cols, width), BF16),
            pltpu.VMEM((heads, width), BF16),
            pltpu.VMEM((1, cols), jnp.int32),
            pltpu.SemaphoreType.DMA((3,)),
        ],
        compiler_params=pltpu.CompilerParams(vmem_limit_bytes=4 << 20),
    )(*given)

    same_core = [
        [CORES * joined(group, sub) + core for group in range(SPLIT) for sub in range(SPLIT)]
        for core in range(CORES)
    ]
    bias = lax.all_to_all(spread, "row", 0, 0, axis_index_groups=same_core, tiled=True)

    bias = bias.reshape(1, SPLIT, 1, depth, width)
    bias = jnp.broadcast_to(bias, (2, SPLIT, 2, depth, width)).reshape(col_size, depth, width)
    send = lax.dynamic_update_slice(send, bias, (0, part, 0))
    block = lax.all_to_all(send, "col", 0, 0, tiled=True)

    swap = [(r, r ^ 1) for r in range(row_size)]
    other = lax.ppermute(block[:, part:], "row", swap)

    made, ahead = pl.pallas_call(
        functools.partial(project_kernel, heads, cols, own_rows),
        out_shape=(
            jax.ShapeDtypeStruct((own_rows + 1, keys_count + queries, 2 * width), BF16),
            jax.ShapeDtypeStruct((heads * queries, keys_count), F32),
        ),
        in_specs=[VMEM, VMEM, VMEM],
        out_specs=(VMEM, VMEM),
        compiler_params=pltpu.CompilerParams(vmem_limit_bytes=12 << 20),
    )(block, w_proj, w_out)

    answer = pl.pallas_call(
        functools.partial(attend_kernel, heads, cols),
        out_shape=jax.ShapeDtypeStruct((SPLIT, own_rows, cols, width), BF16),
        in_specs=[VMEM, VMEM, VMEM, VMEM],
        out_specs=VMEM,
        scratch_shapes=[pltpu.VMEM((heads, SPLIT, CORES, depth // SPLIT, keys_count), F32)],
        compiler_params=pltpu.CompilerParams(vmem_limit_bytes=12 << 20),
    )(block, other, made, ahead)

    near = [[joined(group, sub) for sub in range(SPLIT)] for group in range(SPLIT)]
    answer = answer.reshape(rows, cols, width)
    return lax.all_to_all(answer, "col", 0, 0, axis_index_groups=near, tiled=True)


def solution(mesh):
    in_specs = (P("row", "col", None), P(), P(), P(), P("col"))
    out_specs = P("row", "col", None)
    body = functools.partial(on_device, row_size=mesh.shape["row"], col_size=mesh.shape["col"])
    return jax.shard_map(body, mesh=mesh, in_specs=in_specs, out_specs=out_specs, check_vma=False)
```

```python
import functools

import jax
import jax.numpy as jnp
from jax import lax
from jax.experimental import pallas as pl
from jax.experimental.pallas import tpu as pltpu
from jax.sharding import PartitionSpec as P

F32 = jnp.float32
BF16 = jnp.bfloat16
VMEM = pl.BlockSpec(memory_space=pltpu.VMEM)
HBM = pl.BlockSpec(memory_space=pltpu.HBM)

SPLIT = 4
CORES = 2
PAIR = 4


def joined(group, sub):
    return sub // 2 * 2 * SPLIT + group * 2 + sub % 2


def sub_of(col):
    return col // (2 * SPLIT) * 2 + col % 2


def norm_rows(values):
    center = jnp.mean(values, axis=-1, keepdims=True)
    shifted = values - center
    spread = jnp.mean(shifted * shifted, axis=-1, keepdims=True)
    return (shifted * lax.rsqrt(spread + 1e-05)).astype(BF16)


def norm_kernel(
    rows, cols, pair_hbm, w_bias_hbm, mask_hbm, send_ref, spread_ref, pair_ref, w_bias_ref, mask_ref, read
):
    sources = (pair_hbm, w_bias_hbm, mask_hbm)
    targets = (pair_ref, w_bias_ref, mask_ref)
    copies = [
        pltpu.make_async_copy(source, target, read.at[place])
        for place, (source, target) in enumerate(zip(sources, targets))
    ]
    for copy in copies:
        copy.start()
    copies[0].wait()
    normed = norm_rows(pair_ref[...].astype(F32))
    part = normed.shape[0] // SPLIT
    for member in range(send_ref.shape[0]):
        sub = sub_of(member)
        send_ref[member, 0:part] = normed[sub * part : (sub + 1) * part]

    copies[1].wait()
    copies[2].wait()
    heads, width = w_bias_ref.shape
    head_of_row = lax.broadcasted_iota(jnp.int32, (width, width), 0) // cols
    w_bias = w_bias_ref[...].astype(F32)
    wide = jnp.zeros((width, width), F32)
    for head in range(heads):
        wide = jnp.where(head_of_row == head, w_bias[head : head + 1], wide)
    product = lax.dot_general(
        normed, wide.astype(BF16), (((1,), (1,)), ((), ())), preferred_element_type=F32
    )
    column = lax.broadcasted_iota(jnp.int32, product.shape, 0) % cols
    place = lax.broadcasted_iota(jnp.int32, product.shape, 1) % cols
    product = jnp.where(column == place, product, 0.0)
    bias = jnp.sum(product.reshape(rows, cols, width), axis=1).astype(BF16)
    masked = (mask_ref[...].astype(F32) - 1.0) * 1e9
    masked = jnp.concatenate([masked] * heads, axis=1)
    bias = (bias.astype(F32) + masked).astype(BF16)
    for member in range(spread_ref.shape[0]):
        spread_ref[member] = bias


def project(heads, cols, own_rows, block_ref, w_proj_ref, w_out_ref, made_ref):
    members, _, width = block_ref.shape
    head_size = width // heads
    keys_count = members * cols
    queries = SPLIT * cols
    tall = cols // CORES
    first = lax.axis_index("col") // 2 % SPLIT * 2
    for row in range(own_rows):
        entries = block_ref[:, row * cols : (row + 1) * cols].reshape(keys_count, width)
        made_ref[row, :keys_count] = jnp.dot(
            entries, w_proj_ref[:, width : 3 * width], preferred_element_type=F32
        ).astype(BF16)
        asking = [
            block_ref[pl.ds(first + start, 2), row * cols + core * tall : row * cols + (core + 1) * tall]
            for core in range(CORES)
            for start in (0, 2 * SPLIT)
        ]
        asking = jnp.concatenate(asking, axis=0).reshape(queries, width)
        query = jnp.dot(asking, w_proj_ref[:, :width], preferred_element_type=F32)
        made_ref[row, keys_count:, :width] = (query * head_size ** (-0.5)).astype(BF16)
        gates = jnp.dot(asking, w_proj_ref[:, 3 * width :], preferred_element_type=F32)
        made_ref[row, keys_count:, width:] = gates.astype(BF16)
    made_ref[own_rows, :width, :width] = w_out_ref[...]


def attend(heads, cols, core, source_ref, made_ref, out_ref, bias_ref):
    members, chunk, width = source_ref.shape
    depth = bias_ref.shape[1]
    own_rows = made_ref.shape[0] - 1
    keys_count = members * cols
    group = width // cols
    tall = depth // SPLIT
    lane_head = lax.broadcasted_iota(jnp.int32, (1, width), 1) // (width // heads)
    asking = pl.ds(pl.multiple_of(keys_count + core * depth, depth), depth)

    def products(row):
        query = made_ref[row, asking, :width].astype(F32)
        wide = [jnp.where(lane_head == head, query, 0.0).astype(BF16) for head in range(heads)]
        return lax.dot_general(
            jnp.concatenate(wide, axis=0),
            made_ref[row, :keys_count, :width],
            (((1,), (1,)), ((), ())),
            preferred_element_type=F32,
        )

    ahead = products(0)
    segment = lax.broadcasted_iota(jnp.int32, (1, width), 1) // cols
    for turn in range(members // group):
        turned = []
        for piece in range(group):
            value = source_ref[turn * group + piece, chunk - depth :].astype(F32)
            turned.append([value] + [pltpu.roll(value, cols * d, 1) for d in range(1, group)])
        for head in range(heads):
            value = turned[0][-head % group]
            for piece in range(1, group):
                value = jnp.where(segment == piece, turned[piece][(piece - head) % group], value)
            bias_ref[head, :, turn * width : (turn + 1) * width] = value

    w_out = made_ref[own_rows, :width, :width]
    ones = jnp.ones((keys_count, width), BF16)
    gated = []
    for row in range(own_rows):
        scores = ahead
        if row + 1 < own_rows:
            ahead = products(row + 1)
        values = jnp.concatenate([made_ref[row, :keys_count, width:], ones], axis=1)
        weights = []
        for head in range(heads):
            value = scores[head * depth : (head + 1) * depth] + bias_ref[head]
            top = jnp.max(value, axis=-1, keepdims=True)
            weights.append(jnp.exp(value - top).astype(BF16))
        above = jnp.zeros((depth, width), F32)
        below = jnp.zeros((depth, width), F32)
        for pair in range(0, heads, PAIR):
            both = jnp.concatenate(weights[pair : pair + PAIR], axis=0)
            sums = jnp.dot(both, values, preferred_element_type=F32)
            for head in range(pair, pair + PAIR):
                chosen = slice((head - pair) * depth, (head - pair + 1) * depth)
                above = jnp.where(lane_head == head, sums[chosen, :width], above)
                below = jnp.where(lane_head == head, sums[chosen, width:], below)
        gates = made_ref[row, asking, width:].astype(F32)
        gated.append((above / below * jax.nn.sigmoid(gates)).astype(BF16))
    result = jnp.dot(jnp.concatenate(gated, axis=0), w_out, preferred_element_type=F32).astype(BF16)
    place = pl.ds(pl.multiple_of(core * tall, tall), tall)
    for row in range(own_rows):
        for sub in range(SPLIT):
            start = row * depth + sub * tall
            out_ref[sub, row, place] = result[start : start + tall]


def own_kernel(heads, cols, own_rows, block_ref, w_proj_ref, w_out_ref, made_ref, out_ref, bias_ref):
    project(heads, cols, own_rows, block_ref, w_proj_ref, w_out_ref, made_ref)
    core = lax.axis_index("row") % CORES
    attend(heads, cols, core, block_ref, made_ref, out_ref, bias_ref)


def other_kernel(heads, cols, other_ref, made_ref, half_ref, out_ref, bias_ref):
    del half_ref
    core = 1 - lax.axis_index("row") % CORES
    attend(heads, cols, core, other_ref, made_ref, out_ref, bias_ref)


def on_device(pair, w_proj, w_bias, w_out, token_mask, *, row_size, col_size):
    rows, cols, width = pair.shape
    heads = w_bias.shape[1]
    own_rows = rows // SPLIT
    half = row_size // CORES
    queries = SPLIT * cols
    keys_count = col_size * cols
    depth = queries // CORES
    part = own_rows * cols

    given = (pair.reshape(rows * cols, width), w_bias.T, token_mask[None])
    given = [pltpu.with_memory_space_constraint(array, pltpu.HBM) for array in given]
    send, spread = pl.pallas_call(
        functools.partial(norm_kernel, rows, cols),
        out_shape=(
            jax.ShapeDtypeStruct((col_size, part + depth, width), BF16),
            jax.ShapeDtypeStruct((half, rows, width), BF16),
        ),
        in_specs=[HBM, HBM, HBM],
        out_specs=(VMEM, VMEM),
        scratch_shapes=[
            pltpu.VMEM((rows * cols, width), BF16),
            pltpu.VMEM((heads, width), BF16),
            pltpu.VMEM((1, cols), jnp.int32),
            pltpu.SemaphoreType.DMA((3,)),
        ],
        compiler_params=pltpu.CompilerParams(vmem_limit_bytes=4 << 20),
    )(*given)

    same_core = [
        [CORES * joined(group, sub) + core for group in range(SPLIT) for sub in range(SPLIT)]
        for core in range(CORES)
    ]
    bias = lax.all_to_all(spread, "row", 0, 0, axis_index_groups=same_core, tiled=True)

    bias = bias.reshape(1, SPLIT, 1, depth, width)
    bias = jnp.broadcast_to(bias, (2, SPLIT, 2, depth, width)).reshape(col_size, depth, width)
    send = lax.dynamic_update_slice(send, bias, (0, part, 0))
    block = lax.all_to_all(send, "col", 0, 0, tiled=True)

    swap = [(r, r ^ 1) for r in range(row_size)]
    other = lax.ppermute(block[:, part:], "row", swap)

    made_shape = jax.ShapeDtypeStruct((own_rows + 1, keys_count + queries, 2 * width), BF16)
    answer_shape = jax.ShapeDtypeStruct((SPLIT, own_rows, cols, width), BF16)
    scratch = [pltpu.VMEM((heads, depth, keys_count), F32)]
    params = pltpu.CompilerParams(vmem_limit_bytes=12 << 20)
    made, answer = pl.pallas_call(
        functools.partial(own_kernel, heads, cols, own_rows),
        out_shape=(made_shape, answer_shape),
        in_specs=[VMEM, VMEM, VMEM],
        out_specs=(VMEM, VMEM),
        scratch_shapes=scratch,
        compiler_params=params,
    )(block, w_proj, w_out)
    answer = pl.pallas_call(
        functools.partial(other_kernel, heads, cols),
        out_shape=answer_shape,
        in_specs=[VMEM, VMEM, VMEM],
        out_specs=VMEM,
        scratch_shapes=scratch,
        input_output_aliases={2: 0},
        compiler_params=params,
    )(other, made, answer)

    near = [[joined(group, sub) for sub in range(SPLIT)] for group in range(SPLIT)]
    answer = answer.reshape(rows, cols, width)
    return lax.all_to_all(answer, "col", 0, 0, axis_index_groups=near, tiled=True)


def solution(mesh):
    in_specs = (P("row", "col", None), P(), P(), P(), P("col"))
    out_specs = P("row", "col", None)
    body = functools.partial(on_device, row_size=mesh.shape["row"], col_size=mesh.shape["col"])
    return jax.shard_map(body, mesh=mesh, in_specs=in_specs, out_specs=out_specs, check_vma=False)
```

```python
import functools

import jax
import jax.numpy as jnp
from jax import lax
from jax.experimental import pallas as pl
from jax.experimental.pallas import tpu as pltpu
from jax.sharding import PartitionSpec as P

F32 = jnp.float32
BF16 = jnp.bfloat16
VMEM = pl.BlockSpec(memory_space=pltpu.VMEM)
HBM = pl.BlockSpec(memory_space=pltpu.HBM)

SPLIT = 4
CORES = 2
PAIR = 4


def joined(group, sub):
    return sub // 2 * 2 * SPLIT + group * 2 + sub % 2


def sub_of(col):
    return col // (2 * SPLIT) * 2 + col % 2


def norm_rows(values):
    center = jnp.mean(values, axis=-1, keepdims=True)
    shifted = values - center
    spread = jnp.mean(shifted * shifted, axis=-1, keepdims=True)
    return (shifted * lax.rsqrt(spread + 1e-05)).astype(BF16)


def norm_kernel(
    rows, cols, pair_hbm, w_bias_hbm, mask_hbm, send_ref, spread_ref, pair_ref, w_bias_ref, mask_ref, normed_ref, read
):
    sources = (pair_hbm, w_bias_hbm, mask_hbm)
    targets = (pair_ref, w_bias_ref, mask_ref)
    copies = [
        pltpu.make_async_copy(source, target, read.at[place])
        for place, (source, target) in enumerate(zip(sources, targets))
    ]
    for copy in copies:
        copy.start()
    copies[0].wait()
    normed = norm_rows(pair_ref[...].astype(F32))
    normed_ref[...] = normed
    part = normed.shape[0] // SPLIT
    flip = lax.axis_index("row") % CORES
    for sub in range(SPLIT):
        start = pl.multiple_of(((sub // 2 + flip) % 2 * 2 + sub % 2) * part, part)
        piece = normed_ref[pl.ds(start, part)]
        for member in range(send_ref.shape[0]):
            if sub_of(member) == sub:
                send_ref[member, 0:part] = piece

    copies[1].wait()
    copies[2].wait()
    heads, width = w_bias_ref.shape
    head_of_row = lax.broadcasted_iota(jnp.int32, (width, width), 0) // cols
    w_bias = w_bias_ref[...].astype(F32)
    wide = jnp.zeros((width, width), F32)
    for head in range(heads):
        wide = jnp.where(head_of_row == head, w_bias[head : head + 1], wide)
    product = lax.dot_general(
        normed, wide.astype(BF16), (((1,), (1,)), ((), ())), preferred_element_type=F32
    )
    column = lax.broadcasted_iota(jnp.int32, product.shape, 0) % cols
    place = lax.broadcasted_iota(jnp.int32, product.shape, 1) % cols
    product = jnp.where(column == place, product, 0.0)
    bias = jnp.sum(product.reshape(rows, cols, width), axis=1).astype(BF16)
    masked = (mask_ref[...].astype(F32) - 1.0) * 1e9
    masked = jnp.concatenate([masked] * heads, axis=1)
    bias = (bias.astype(F32) + masked).astype(BF16)
    for member in range(spread_ref.shape[0]):
        spread_ref[member] = bias


def project(heads, cols, own_rows, block_ref, w_proj_ref, w_out_ref, made_ref):
    members, _, width = block_ref.shape
    head_size = width // heads
    keys_count = members * cols
    queries = SPLIT * cols
    tall = cols // CORES
    first = lax.axis_index("col") // 2 % SPLIT * 2
    flip = lax.axis_index("row") % CORES
    for row in range(own_rows):
        entries = block_ref[:, row * cols : (row + 1) * cols].reshape(keys_count, width)
        made_ref[row, :keys_count] = jnp.dot(
            entries, w_proj_ref[:, width : 3 * width], preferred_element_type=F32
        ).astype(BF16)
        asking = [
            block_ref[pl.ds(first + (high + flip) % 2 * (2 * SPLIT), 2), row * cols + core * tall : row * cols + (core + 1) * tall]
            for core in range(CORES)
            for high in range(2)
        ]
        asking = jnp.concatenate(asking, axis=0).reshape(queries, width)
        query = jnp.dot(asking, w_proj_ref[:, :width], preferred_element_type=F32)
        made_ref[row, keys_count:, :width] = (query * head_size ** (-0.5)).astype(BF16)
        gates = jnp.dot(asking, w_proj_ref[:, 3 * width :], preferred_element_type=F32)
        made_ref[row, keys_count:, width:] = gates.astype(BF16)
    made_ref[own_rows, :width, :width] = w_out_ref[...]


def attend(heads, cols, core, shift, source_ref, made_ref, out_ref, bias_ref):
    members, chunk, width = source_ref.shape
    depth = bias_ref.shape[1]
    own_rows = made_ref.shape[0] - 1
    keys_count = members * cols
    group = width // cols
    tall = depth // SPLIT
    lane_head = lax.broadcasted_iota(jnp.int32, (1, width), 1) // (width // heads)
    asking = pl.ds(pl.multiple_of(keys_count + core * depth, depth), depth)

    def products(row):
        query = made_ref[row, asking, :width].astype(F32)
        wide = [jnp.where(lane_head == head, query, 0.0).astype(BF16) for head in range(heads)]
        return lax.dot_general(
            jnp.concatenate(wide, axis=0),
            made_ref[row, :keys_count, :width],
            (((1,), (1,)), ((), ())),
            preferred_element_type=F32,
        )

    ahead = products(0)
    segment = lax.broadcasted_iota(jnp.int32, (1, width), 1) // cols
    for turn in range(members // group):
        turned = []
        for piece in range(group):
            member = (turn * group + piece + shift) % members
            value = source_ref[member, chunk - depth :].astype(F32)
            turned.append([value] + [pltpu.roll(value, cols * d, 1) for d in range(1, group)])
        for head in range(heads):
            value = turned[0][-head % group]
            for piece in range(1, group):
                value = jnp.where(segment == piece, turned[piece][(piece - head) % group], value)
            bias_ref[head, :, turn * width : (turn + 1) * width] = value

    w_out = made_ref[own_rows, :width, :width]
    ones = jnp.ones((keys_count, width), BF16)
    gated = []
    for row in range(own_rows):
        scores = ahead
        if row + 1 < own_rows:
            ahead = products(row + 1)
        values = jnp.concatenate([made_ref[row, :keys_count, width:], ones], axis=1)
        weights = []
        for head in range(heads):
            value = scores[head * depth : (head + 1) * depth] + bias_ref[head]
            top = jnp.max(value, axis=-1, keepdims=True)
            weights.append(jnp.exp(value - top).astype(BF16))
        above = jnp.zeros((depth, width), F32)
        below = jnp.zeros((depth, width), F32)
        for pair in range(0, heads, PAIR):
            both = jnp.concatenate(weights[pair : pair + PAIR], axis=0)
            sums = jnp.dot(both, values, preferred_element_type=F32)
            for head in range(pair, pair + PAIR):
                chosen = slice((head - pair) * depth, (head - pair + 1) * depth)
                above = jnp.where(lane_head == head, sums[chosen, :width], above)
                below = jnp.where(lane_head == head, sums[chosen, width:], below)
        gates = made_ref[row, asking, width:].astype(F32)
        gated.append((above / below * jax.nn.sigmoid(gates)).astype(BF16))
    result = jnp.dot(jnp.concatenate(gated, axis=0), w_out, preferred_element_type=F32).astype(BF16)
    place = pl.ds(pl.multiple_of(core * tall, tall), tall)
    for row in range(own_rows):
        for sub in range(SPLIT):
            start = row * depth + sub * tall
            out_ref[sub, row, place] = result[start : start + tall]


def own_kernel(heads, cols, own_rows, block_ref, w_proj_ref, w_out_ref, made_ref, out_ref, bias_ref):
    project(heads, cols, own_rows, block_ref, w_proj_ref, w_out_ref, made_ref)
    core = lax.axis_index("row") % CORES
    attend(heads, cols, core, 0, block_ref, made_ref, out_ref, bias_ref)


def other_kernel(heads, cols, other_ref, made_ref, half_ref, out_ref, bias_ref):
    del half_ref
    core = 1 - lax.axis_index("row") % CORES
    attend(heads, cols, core, other_ref.shape[0] // 2, other_ref, made_ref, out_ref, bias_ref)


def on_device(pair, w_proj, w_bias, w_out, token_mask, *, row_size, col_size):
    rows, cols, width = pair.shape
    heads = w_bias.shape[1]
    own_rows = rows // SPLIT
    half = row_size // CORES
    queries = SPLIT * cols
    keys_count = col_size * cols
    depth = queries // CORES
    part = own_rows * cols

    given = (pair.reshape(rows * cols, width), w_bias.T, token_mask[None])
    given = [pltpu.with_memory_space_constraint(array, pltpu.HBM) for array in given]
    send, spread = pl.pallas_call(
        functools.partial(norm_kernel, rows, cols),
        out_shape=(
            jax.ShapeDtypeStruct((col_size, part + depth, width), BF16),
            jax.ShapeDtypeStruct((half, rows, width), BF16),
        ),
        in_specs=[HBM, HBM, HBM],
        out_specs=(VMEM, VMEM),
        scratch_shapes=[
            pltpu.VMEM((rows * cols, width), BF16),
            pltpu.VMEM((heads, width), BF16),
            pltpu.VMEM((1, cols), jnp.int32),
            pltpu.VMEM((rows * cols, width), BF16),
            pltpu.SemaphoreType.DMA((3,)),
        ],
        compiler_params=pltpu.CompilerParams(vmem_limit_bytes=4 << 20),
    )(*given)

    same_core = [
        [CORES * joined(group, sub) + core for group in range(SPLIT) for sub in range(SPLIT)]
        for core in range(CORES)
    ]
    bias = lax.all_to_all(spread, "row", 0, 0, axis_index_groups=same_core, tiled=True)

    bias = bias.reshape(1, SPLIT, 1, depth, width)
    bias = jnp.broadcast_to(bias, (2, SPLIT, 2, depth, width)).reshape(col_size, depth, width)
    send = lax.dynamic_update_slice(send, bias, (0, part, 0))
    orders = [
        [row * col_size + (col + row % CORES * (col_size // 2)) % col_size for col in range(col_size)]
        for row in range(row_size)
    ]
    block = lax.all_to_all(send, ("row", "col"), 0, 0, axis_index_groups=orders, tiled=True)

    swap = [(r, r ^ 1) for r in range(row_size)]
    other = lax.ppermute(block[:, part:], "row", swap)

    made_shape = jax.ShapeDtypeStruct((own_rows + 1, keys_count + queries, 2 * width), BF16)
    answer_shape = jax.ShapeDtypeStruct((SPLIT, own_rows, cols, width), BF16)
    scratch = [pltpu.VMEM((heads, depth, keys_count), F32)]
    params = pltpu.CompilerParams(vmem_limit_bytes=12 << 20)
    made, answer = pl.pallas_call(
        functools.partial(own_kernel, heads, cols, own_rows),
        out_shape=(made_shape, answer_shape),
        in_specs=[VMEM, VMEM, VMEM],
        out_specs=(VMEM, VMEM),
        scratch_shapes=scratch,
        compiler_params=params,
    )(block, w_proj, w_out)
    answer = pl.pallas_call(
        functools.partial(other_kernel, heads, cols),
        out_shape=answer_shape,
        in_specs=[VMEM, VMEM, VMEM],
        out_specs=VMEM,
        scratch_shapes=scratch,
        input_output_aliases={2: 0},
        compiler_params=params,
    )(other, made, answer)

    near = [[joined(group, sub) for sub in range(SPLIT)] for group in range(SPLIT)]
    answer = answer.reshape(rows, cols, width)
    return lax.all_to_all(answer, "col", 0, 0, axis_index_groups=near, tiled=True)


def solution(mesh):
    in_specs = (P("row", "col", None), P(), P(), P(), P("col"))
    out_specs = P("row", "col", None)
    body = functools.partial(on_device, row_size=mesh.shape["row"], col_size=mesh.shape["col"])
    return jax.shard_map(body, mesh=mesh, in_specs=in_specs, out_specs=out_specs, check_vma=False)
```

```python
import functools

import jax
import jax.numpy as jnp
from jax import lax
from jax.experimental import pallas as pl
from jax.experimental.pallas import tpu as pltpu
from jax.sharding import PartitionSpec as P

F32 = jnp.float32
BF16 = jnp.bfloat16
VMEM = pl.BlockSpec(memory_space=pltpu.VMEM)
HBM = pl.BlockSpec(memory_space=pltpu.HBM)

SPLIT = 4
CORES = 2
PAIR = 4


def joined(group, sub):
    return sub // 2 * 2 * SPLIT + group * 2 + sub % 2


def sub_of(col):
    return col // (2 * SPLIT) * 2 + col % 2


def norm_rows(values):
    center = jnp.mean(values, axis=-1, keepdims=True)
    shifted = values - center
    spread = jnp.mean(shifted * shifted, axis=-1, keepdims=True)
    return (shifted * lax.rsqrt(spread + 1e-05)).astype(BF16)


def norm_kernel(
    rows, cols, pair_hbm, w_bias_hbm, mask_hbm, send_ref, spread_ref, pair_ref, w_bias_ref, mask_ref, read
):
    sources = (pair_hbm, w_bias_hbm, mask_hbm)
    targets = (pair_ref, w_bias_ref, mask_ref)
    copies = [
        pltpu.make_async_copy(source, target, read.at[place])
        for place, (source, target) in enumerate(zip(sources, targets))
    ]
    for copy in copies:
        copy.start()
    copies[0].wait()
    normed = norm_rows(pair_ref[...].astype(F32))
    part = normed.shape[0] // SPLIT
    for member in range(send_ref.shape[0]):
        sub = sub_of(member)
        send_ref[member, 0:part] = normed[sub * part : (sub + 1) * part]

    copies[1].wait()
    copies[2].wait()
    heads, width = w_bias_ref.shape
    head_of_row = lax.broadcasted_iota(jnp.int32, (width, width), 0) // cols
    w_bias = w_bias_ref[...].astype(F32)
    wide = jnp.zeros((width, width), F32)
    for head in range(heads):
        wide = jnp.where(head_of_row == head, w_bias[head : head + 1], wide)
    product = lax.dot_general(
        normed, wide.astype(BF16), (((1,), (1,)), ((), ())), preferred_element_type=F32
    )
    column = lax.broadcasted_iota(jnp.int32, product.shape, 0) % cols
    place = lax.broadcasted_iota(jnp.int32, product.shape, 1) % cols
    product = jnp.where(column == place, product, 0.0)
    bias = jnp.sum(product.reshape(rows, cols, width), axis=1).astype(BF16)
    masked = (mask_ref[...].astype(F32) - 1.0) * 1e9
    masked = jnp.concatenate([masked] * heads, axis=1)
    bias = (bias.astype(F32) + masked).astype(BF16)
    for member in range(spread_ref.shape[0]):
        spread_ref[member] = bias


def project(heads, cols, own_rows, block_ref, w_proj_ref, made_ref):
    members, _, width = block_ref.shape
    head_size = width // heads
    keys_count = members * cols
    queries = SPLIT * cols
    tall = cols // CORES
    first = lax.axis_index("col") // 2 % SPLIT * 2
    for row in range(own_rows):
        entries = block_ref[:, row * cols : (row + 1) * cols].reshape(keys_count, width)
        made_ref[row, :keys_count] = jnp.dot(
            entries, w_proj_ref[:, width : 3 * width], preferred_element_type=F32
        ).astype(BF16)
        asking = [
            block_ref[pl.ds(first + start, 2), row * cols + core * tall : row * cols + (core + 1) * tall]
            for core in range(CORES)
            for start in (0, 2 * SPLIT)
        ]
        asking = jnp.concatenate(asking, axis=0).reshape(queries, width)
        query = jnp.dot(asking, w_proj_ref[:, :width], preferred_element_type=F32)
        made_ref[row, keys_count:, :width] = (query * head_size ** (-0.5)).astype(BF16)
        gates = jnp.dot(asking, w_proj_ref[:, 3 * width :], preferred_element_type=F32)
        made_ref[row, keys_count:, width:] = gates.astype(BF16)


def attend(heads, cols, core, source_ref, made_ref, out_ref, bias_ref):
    members, chunk, width = source_ref.shape
    depth = bias_ref.shape[1]
    own_rows = made_ref.shape[0]
    keys_count = members * cols
    group = width // cols
    tall = depth // SPLIT
    lane_head = lax.broadcasted_iota(jnp.int32, (1, width), 1) // (width // heads)
    asking = pl.ds(pl.multiple_of(keys_count + core * depth, depth), depth)

    def products(row):
        query = made_ref[row, asking, :width].astype(F32)
        wide = [jnp.where(lane_head == head, query, 0.0).astype(BF16) for head in range(heads)]
        return lax.dot_general(
            jnp.concatenate(wide, axis=0),
            made_ref[row, :keys_count, :width],
            (((1,), (1,)), ((), ())),
            preferred_element_type=F32,
        )

    ahead = products(0)
    segment = lax.broadcasted_iota(jnp.int32, (1, width), 1) // cols
    for turn in range(members // group):
        turned = []
        for piece in range(group):
            value = source_ref[turn * group + piece, chunk - depth :].astype(F32)
            turned.append([value] + [pltpu.roll(value, cols * d, 1) for d in range(1, group)])
        for head in range(heads):
            value = turned[0][-head % group]
            for piece in range(1, group):
                value = jnp.where(segment == piece, turned[piece][(piece - head) % group], value)
            bias_ref[head, :, turn * width : (turn + 1) * width] = value

    ones = jnp.ones((keys_count, width), BF16)
    gated = []
    for row in range(own_rows):
        scores = ahead
        if row + 1 < own_rows:
            ahead = products(row + 1)
        values = jnp.concatenate([made_ref[row, :keys_count, width:], ones], axis=1)
        weights = []
        for head in range(heads):
            value = scores[head * depth : (head + 1) * depth] + bias_ref[head]
            top = jnp.max(value, axis=-1, keepdims=True)
            weights.append(jnp.exp(value - top).astype(BF16))
        above = jnp.zeros((depth, width), F32)
        below = jnp.zeros((depth, width), F32)
        for pair in range(0, heads, PAIR):
            both = jnp.concatenate(weights[pair : pair + PAIR], axis=0)
            sums = jnp.dot(both, values, preferred_element_type=F32)
            for head in range(pair, pair + PAIR):
                chosen = slice((head - pair) * depth, (head - pair + 1) * depth)
                above = jnp.where(lane_head == head, sums[chosen, :width], above)
                below = jnp.where(lane_head == head, sums[chosen, width:], below)
        gates = made_ref[row, asking, width:].astype(F32)
        gated.append((above / below * jax.nn.sigmoid(gates)).astype(BF16))
    place = pl.ds(pl.multiple_of(core * tall, tall), tall)
    for row in range(own_rows):
        for sub in range(SPLIT):
            out_ref[sub, row, place] = gated[row][sub * tall : (sub + 1) * tall]


def own_kernel(heads, cols, own_rows, block_ref, w_proj_ref, made_ref, out_ref, bias_ref):
    project(heads, cols, own_rows, block_ref, w_proj_ref, made_ref)
    core = lax.axis_index("row") % CORES
    attend(heads, cols, core, block_ref, made_ref, out_ref, bias_ref)


def other_kernel(heads, cols, other_ref, made_ref, half_ref, out_ref, bias_ref):
    del half_ref
    core = 1 - lax.axis_index("row") % CORES
    attend(heads, cols, core, other_ref, made_ref, out_ref, bias_ref)


def update_kernel(gated_ref, w_out_ref, out_ref):
    out_ref[...] = jnp.dot(gated_ref[...], w_out_ref[...], preferred_element_type=F32).astype(BF16)


def on_device(pair, w_proj, w_bias, w_out, token_mask, *, row_size, col_size):
    rows, cols, width = pair.shape
    heads = w_bias.shape[1]
    own_rows = rows // SPLIT
    half = row_size // CORES
    queries = SPLIT * cols
    keys_count = col_size * cols
    depth = queries // CORES
    part = own_rows * cols

    given = (pair.reshape(rows * cols, width), w_bias.T, token_mask[None])
    given = [pltpu.with_memory_space_constraint(array, pltpu.HBM) for array in given]
    send, spread = pl.pallas_call(
        functools.partial(norm_kernel, rows, cols),
        out_shape=(
            jax.ShapeDtypeStruct((col_size, part + depth, width), BF16),
            jax.ShapeDtypeStruct((half, rows, width), BF16),
        ),
        in_specs=[HBM, HBM, HBM],
        out_specs=(VMEM, VMEM),
        scratch_shapes=[
            pltpu.VMEM((rows * cols, width), BF16),
            pltpu.VMEM((heads, width), BF16),
            pltpu.VMEM((1, cols), jnp.int32),
            pltpu.SemaphoreType.DMA((3,)),
        ],
        compiler_params=pltpu.CompilerParams(vmem_limit_bytes=4 << 20),
    )(*given)

    same_core = [
        [CORES * joined(group, sub) + core for group in range(SPLIT) for sub in range(SPLIT)]
        for core in range(CORES)
    ]
    bias = lax.all_to_all(spread, "row", 0, 0, axis_index_groups=same_core, tiled=True)

    bias = bias.reshape(1, SPLIT, 1, depth, width)
    bias = jnp.broadcast_to(bias, (2, SPLIT, 2, depth, width)).reshape(col_size, depth, width)
    send = lax.dynamic_update_slice(send, bias, (0, part, 0))
    block = lax.all_to_all(send, "col", 0, 0, tiled=True)

    swap = [(r, r ^ 1) for r in range(row_size)]
    other = lax.ppermute(block[:, part:], "row", swap)

    made_shape = jax.ShapeDtypeStruct((own_rows, keys_count + queries, 2 * width), BF16)
    answer_shape = jax.ShapeDtypeStruct((SPLIT, own_rows, cols, width), BF16)
    scratch = [pltpu.VMEM((heads, depth, keys_count), F32)]
    params = pltpu.CompilerParams(vmem_limit_bytes=12 << 20)
    made, answer = pl.pallas_call(
        functools.partial(own_kernel, heads, cols, own_rows),
        out_shape=(made_shape, answer_shape),
        in_specs=[VMEM, VMEM],
        out_specs=(VMEM, VMEM),
        scratch_shapes=scratch,
        compiler_params=params,
    )(block, w_proj)
    answer = pl.pallas_call(
        functools.partial(other_kernel, heads, cols),
        out_shape=answer_shape,
        in_specs=[VMEM, VMEM, VMEM],
        out_specs=VMEM,
        scratch_shapes=scratch,
        input_output_aliases={2: 0},
        compiler_params=params,
    )(other, made, answer)

    near = [[joined(group, sub) for sub in range(SPLIT)] for group in range(SPLIT)]
    answer = answer.reshape(rows, cols, width)
    back = lax.all_to_all(answer, "col", 0, 0, axis_index_groups=near, tiled=True)
    update = pl.pallas_call(
        update_kernel,
        out_shape=jax.ShapeDtypeStruct((rows * cols, width), BF16),
        in_specs=[VMEM, VMEM],
        out_specs=VMEM,
        compiler_params=pltpu.CompilerParams(vmem_limit_bytes=4 << 20),
    )(back.reshape(rows * cols, width), w_out)
    return update.reshape(rows, cols, width)


def solution(mesh):
    in_specs = (P("row", "col", None), P(), P(), P(), P("col"))
    out_specs = P("row", "col", None)
    body = functools.partial(on_device, row_size=mesh.shape["row"], col_size=mesh.shape["col"])
    return jax.shard_map(body, mesh=mesh, in_specs=in_specs, out_specs=out_specs, check_vma=False)
```

```python
import functools

import jax
import jax.numpy as jnp
from jax import lax
from jax.experimental import pallas as pl
from jax.experimental.pallas import tpu as pltpu
from jax.sharding import PartitionSpec as P

F32 = jnp.float32
BF16 = jnp.bfloat16
VMEM = pl.BlockSpec(memory_space=pltpu.VMEM)
HBM = pl.BlockSpec(memory_space=pltpu.HBM)

SPLIT = 4
CORES = 2
PAIR = 4


def joined(group, sub):
    return sub // 2 * 2 * SPLIT + group * 2 + sub % 2


def sub_of(col):
    return col // (2 * SPLIT) * 2 + col % 2


def norm_rows(values):
    center = jnp.mean(values, axis=-1, keepdims=True)
    shifted = values - center
    spread = jnp.mean(shifted * shifted, axis=-1, keepdims=True)
    return (shifted * lax.rsqrt(spread + 1e-05)).astype(BF16)


def norm_kernel(
    rows, cols, pair_hbm, w_bias_hbm, mask_hbm, send_ref, spread_ref, pair_ref, w_bias_ref, mask_ref, read
):
    sources = (pair_hbm, w_bias_hbm, mask_hbm)
    targets = (pair_ref, w_bias_ref, mask_ref)
    copies = [
        pltpu.make_async_copy(source, target, read.at[place])
        for place, (source, target) in enumerate(zip(sources, targets))
    ]
    for copy in copies:
        copy.start()
    copies[0].wait()
    normed = norm_rows(pair_ref[...].astype(F32))
    part = normed.shape[0] // SPLIT
    for member in range(send_ref.shape[0]):
        sub = sub_of(member)
        send_ref[member, 0:part] = normed[sub * part : (sub + 1) * part]

    copies[1].wait()
    copies[2].wait()
    heads, width = w_bias_ref.shape
    head_of_row = lax.broadcasted_iota(jnp.int32, (width, width), 0) // cols
    w_bias = w_bias_ref[...].astype(F32)
    wide = jnp.zeros((width, width), F32)
    for head in range(heads):
        wide = jnp.where(head_of_row == head, w_bias[head : head + 1], wide)
    product = lax.dot_general(
        normed, wide.astype(BF16), (((1,), (1,)), ((), ())), preferred_element_type=F32
    )
    column = lax.broadcasted_iota(jnp.int32, product.shape, 0) % cols
    place = lax.broadcasted_iota(jnp.int32, product.shape, 1) % cols
    product = jnp.where(column == place, product, 0.0)
    bias = jnp.sum(product.reshape(rows, cols, width), axis=1).astype(BF16)
    masked = (mask_ref[...].astype(F32) - 1.0) * 1e9
    masked = jnp.concatenate([masked] * heads, axis=1)
    bias = (bias.astype(F32) + masked).astype(BF16)
    for member in range(spread_ref.shape[0]):
        spread_ref[member] = bias


def project(heads, cols, own_rows, block_ref, w_proj_ref, made_ref):
    members, _, width = block_ref.shape
    head_size = width // heads
    keys_count = members * cols
    queries = SPLIT * cols
    tall = cols // CORES
    first = lax.axis_index("col") // 2 % SPLIT * 2
    for row in range(own_rows):
        entries = block_ref[:, row * cols : (row + 1) * cols].reshape(keys_count, width)
        made_ref[row, :keys_count] = jnp.dot(
            entries, w_proj_ref[:, width : 3 * width], preferred_element_type=F32
        ).astype(BF16)
        asking = [
            block_ref[pl.ds(first + start, 2), row * cols + core * tall : row * cols + (core + 1) * tall]
            for core in range(CORES)
            for start in (0, 2 * SPLIT)
        ]
        asking = jnp.concatenate(asking, axis=0).reshape(queries, width)
        query = jnp.dot(asking, w_proj_ref[:, :width], preferred_element_type=F32)
        made_ref[row, keys_count:, :width] = (query * head_size ** (-0.5)).astype(BF16)
        gates = jnp.dot(asking, w_proj_ref[:, 3 * width :], preferred_element_type=F32)
        made_ref[row, keys_count:, width:] = gates.astype(BF16)


def attend(heads, cols, core, source_ref, made_ref, out_ref, bias_ref):
    members, chunk, width = source_ref.shape
    depth = bias_ref.shape[1]
    own_rows = made_ref.shape[0]
    keys_count = members * cols
    group = width // cols
    tall = depth // SPLIT
    lane_head = lax.broadcasted_iota(jnp.int32, (1, width), 1) // (width // heads)
    asking = pl.ds(pl.multiple_of(keys_count + core * depth, depth), depth)

    def products(row):
        query = made_ref[row, asking, :width].astype(F32)
        wide = [jnp.where(lane_head == head, query, 0.0).astype(BF16) for head in range(heads)]
        return lax.dot_general(
            jnp.concatenate(wide, axis=0),
            made_ref[row, :keys_count, :width],
            (((1,), (1,)), ((), ())),
            preferred_element_type=F32,
        )

    ahead = products(0)
    segment = lax.broadcasted_iota(jnp.int32, (1, width), 1) // cols
    for turn in range(members // group):
        turned = []
        for piece in range(group):
            value = source_ref[turn * group + piece, chunk - depth :].astype(F32)
            turned.append([value] + [pltpu.roll(value, cols * d, 1) for d in range(1, group)])
        for head in range(heads):
            value = turned[0][-head % group]
            for piece in range(1, group):
                value = jnp.where(segment == piece, turned[piece][(piece - head) % group], value)
            bias_ref[head, :, turn * width : (turn + 1) * width] = value

    ones = jnp.ones((keys_count, width), BF16)
    gated = []
    for row in range(own_rows):
        scores = ahead
        if row + 1 < own_rows:
            ahead = products(row + 1)
        values = jnp.concatenate([made_ref[row, :keys_count, width:], ones], axis=1)
        weights = []
        for head in range(heads):
            value = scores[head * depth : (head + 1) * depth] + bias_ref[head]
            top = jnp.max(value, axis=-1, keepdims=True)
            weights.append(jnp.exp(value - top).astype(BF16))
        above = jnp.zeros((depth, width), F32)
        below = jnp.zeros((depth, width), F32)
        for pair in range(0, heads, PAIR):
            both = jnp.concatenate(weights[pair : pair + PAIR], axis=0)
            sums = jnp.dot(both, values, preferred_element_type=F32)
            for head in range(pair, pair + PAIR):
                chosen = slice((head - pair) * depth, (head - pair + 1) * depth)
                above = jnp.where(lane_head == head, sums[chosen, :width], above)
                below = jnp.where(lane_head == head, sums[chosen, width:], below)
        gates = made_ref[row, asking, width:].astype(F32)
        gated.append((above / below * jax.nn.sigmoid(gates)).astype(BF16))
    place = pl.ds(pl.multiple_of(core * tall, tall), tall)
    for row in range(own_rows):
        for sub in range(SPLIT):
            out_ref[sub, row, place] = gated[row][sub * tall : (sub + 1) * tall]


def own_kernel(heads, cols, own_rows, block_ref, w_proj_ref, made_ref, out_ref, bias_ref):
    project(heads, cols, own_rows, block_ref, w_proj_ref, made_ref)
    core = lax.axis_index("row") % CORES
    attend(heads, cols, core, block_ref, made_ref, out_ref, bias_ref)


def other_kernel(heads, cols, other_ref, made_ref, half_ref, out_ref, bias_ref):
    del half_ref
    core = 1 - lax.axis_index("row") % CORES
    attend(heads, cols, core, other_ref, made_ref, out_ref, bias_ref)


def update_kernel(gated_ref, w_out_ref, out_hbm, made_ref, sent):
    size = gated_ref.shape[0] // 2
    copies = []
    for half in range(2):
        chosen = slice(half * size, (half + 1) * size)
        result = jnp.dot(gated_ref[chosen], w_out_ref[...], preferred_element_type=F32)
        made_ref[chosen] = result.astype(BF16)
        rows = pl.ds(half * size, size)
        copies.append(pltpu.make_async_copy(made_ref.at[rows], out_hbm.at[rows], sent.at[half]))
        copies[-1].start()
    for copy in copies:
        copy.wait()


def on_device(pair, w_proj, w_bias, w_out, token_mask, *, row_size, col_size):
    rows, cols, width = pair.shape
    heads = w_bias.shape[1]
    own_rows = rows // SPLIT
    half = row_size // CORES
    queries = SPLIT * cols
    keys_count = col_size * cols
    depth = queries // CORES
    part = own_rows * cols

    given = (pair.reshape(rows * cols, width), w_bias.T, token_mask[None])
    given = [pltpu.with_memory_space_constraint(array, pltpu.HBM) for array in given]
    send, spread = pl.pallas_call(
        functools.partial(norm_kernel, rows, cols),
        out_shape=(
            jax.ShapeDtypeStruct((col_size, part + depth, width), BF16),
            jax.ShapeDtypeStruct((half, rows, width), BF16),
        ),
        in_specs=[HBM, HBM, HBM],
        out_specs=(VMEM, VMEM),
        scratch_shapes=[
            pltpu.VMEM((rows * cols, width), BF16),
            pltpu.VMEM((heads, width), BF16),
            pltpu.VMEM((1, cols), jnp.int32),
            pltpu.SemaphoreType.DMA((3,)),
        ],
        compiler_params=pltpu.CompilerParams(vmem_limit_bytes=4 << 20),
    )(*given)

    same_core = [
        [CORES * joined(group, sub) + core for group in range(SPLIT) for sub in range(SPLIT)]
        for core in range(CORES)
    ]
    bias = lax.all_to_all(spread, "row", 0, 0, axis_index_groups=same_core, tiled=True)

    bias = bias.reshape(1, SPLIT, 1, depth, width)
    bias = jnp.broadcast_to(bias, (2, SPLIT, 2, depth, width)).reshape(col_size, depth, width)
    send = lax.dynamic_update_slice(send, bias, (0, part, 0))
    block = lax.all_to_all(send, "col", 0, 0, tiled=True)

    swap = [(r, r ^ 1) for r in range(row_size)]
    other = lax.ppermute(block[:, part:], "row", swap)

    made_shape = jax.ShapeDtypeStruct((own_rows, keys_count + queries, 2 * width), BF16)
    answer_shape = jax.ShapeDtypeStruct((SPLIT, own_rows, cols, width), BF16)
    scratch = [pltpu.VMEM((heads, depth, keys_count), F32)]
    params = pltpu.CompilerParams(vmem_limit_bytes=12 << 20)
    made, answer = pl.pallas_call(
        functools.partial(own_kernel, heads, cols, own_rows),
        out_shape=(made_shape, answer_shape),
        in_specs=[VMEM, VMEM],
        out_specs=(VMEM, VMEM),
        scratch_shapes=scratch,
        compiler_params=params,
    )(block, w_proj)
    answer = pl.pallas_call(
        functools.partial(other_kernel, heads, cols),
        out_shape=answer_shape,
        in_specs=[VMEM, VMEM, VMEM],
        out_specs=VMEM,
        scratch_shapes=scratch,
        input_output_aliases={2: 0},
        compiler_params=params,
    )(other, made, answer)

    near = [[joined(group, sub) for sub in range(SPLIT)] for group in range(SPLIT)]
    answer = answer.reshape(rows, cols, width)
    back = lax.all_to_all(answer, "col", 0, 0, axis_index_groups=near, tiled=True)
    update = pl.pallas_call(
        update_kernel,
        out_shape=jax.ShapeDtypeStruct((rows * cols, width), BF16),
        in_specs=[VMEM, VMEM],
        out_specs=HBM,
        scratch_shapes=[pltpu.VMEM((rows * cols, width), BF16), pltpu.SemaphoreType.DMA((2,))],
        compiler_params=pltpu.CompilerParams(vmem_limit_bytes=4 << 20),
    )(back.reshape(rows * cols, width), w_out)
    return update.reshape(rows, cols, width)


def solution(mesh):
    in_specs = (P("row", "col", None), P(), P(), P(), P("col"))
    out_specs = P("row", "col", None)
    body = functools.partial(on_device, row_size=mesh.shape["row"], col_size=mesh.shape["col"])
    return jax.shard_map(body, mesh=mesh, in_specs=in_specs, out_specs=out_specs, check_vma=False)
```
